512 devices in a mesh: row: 32 (over z_hi, x, core), col: 16 (over y, z_lo).
Axes of the slice: x: 4, y: 8, z: 8 (z_hi: 4, z_lo: 2; z = z_hi * 2 + z_lo), core: 2. Of those that a mesh axis runs over, the one named last changes fastest.
Arguments:
- tile_data: bfloat16 [32, 16, 12, 256, 256], P('row', 'col'), may hold values from -1.5 to 1.5
- tile_list: int32 [3, 32, 16, 12], P(None, 'row', 'col'), may hold values from 0 to 4095, as said below
- tile_count: int32 [32, 16], P('row', 'col'), may hold values from 1 to 12, as said below
- current: float32 [8, 1048576], P(None, ('row', 'col'))
- current_image: float32 [8, 1048576], P(None, ('row', 'col'))
- direction: float32 [8, 1048576], P(None, ('row', 'col'))
- direction_image: float32 [8, 1048576], P(None, ('row', 'col'))
- energies: float32 [1048576], P(('row', 'col')), may hold values from 0.2 to 11
- precond: float32 [1048576], P(('row', 'col')), may hold values from 0.2 to 1
- ritz_prev: float32 [8], replicated, may hold values from 0.5 to 3.5
Outputs:
- applied: float32 [8, 1048576], P(None, ('row', 'col'))
- projected: float32 [24, 24], replicated
The draws below stay inside these ranges and needn't reach their ends.
Inputs may be any that keep to these rules, and one draw needn't show every extreme that they name: `tile_list`: for the device at row index r and col index c, every entry holds a global tile row (component 0) from r * 128 to (r + 1) * 128 - 1, a global tile column (component 1) not above that row whose piece number, column * 256 // 2048, leaves remainder c when divided by 16, and a slot (component 2); the slots of one device are a permutation of 0 to 11. Only a device's first tile_count entries are live. `tile_count`: every device at the last row index has 12 live entries.
All inputs are finite; a program needn't handle non-finite values.
Results may differ from the reference program's by a relative error of at most 0.0003.
Values sent between devices are 32-bit elements; how exact they have to be, the bound alone decides.
A program may use at most 64 MiB of HBM per device.

```python
import math
import jax
import jax.numpy as jnp
from jax import lax

NVEC = 8
B = 256
PIECE = 2048
TILES_DEV = 12
N = 1048576
GRID_ROWS = 32
GRID_COLS = 16


def vector_block(key, salt):
    key = jax.random.fold_in(key, salt)
    key_values, key_rates = jax.random.split(key, 2)
    spot = jnp.arange(N, dtype=jnp.float32) / N
    rates = jax.random.uniform(key_rates, (NVEC, 1), jnp.float32, -2.0, 2.0)
    values = jax.random.normal(key_values, (NVEC, N), jnp.float32)
    return values * jnp.exp(-rates * spot[None, :])


def energy_levels(key):
    key = jax.random.fold_in(key, 29)
    spot = jnp.arange(N, dtype=jnp.float32) / N
    rough = jnp.exp(jax.random.uniform(key, (N,), jnp.float32, -0.7, 0.7))
    return (0.5 + 3.0 * spot) * rough


def draw_current(key, part):
    return vector_block(key, 101)


def draw_current_image(key, part):
    base = vector_block(key, 101) * energy_levels(key)[None, :]
    key = jax.random.fold_in(key, 7)
    return base + 0.3 * jax.random.normal(key, (NVEC, N), jnp.float32)


def draw_direction(key, part):
    return vector_block(key, 202)


def draw_direction_image(key, part):
    base = vector_block(key, 202) * energy_levels(key)[None, :]
    key = jax.random.fold_in(key, 8)
    return base + 0.3 * jax.random.normal(key, (NVEC, N), jnp.float32)


def draw_energies(key, part):
    return energy_levels(key)


def draw_tile_list(key, part):
    key = jax.random.fold_in(key, 3)
    key_row, key_piece, key_sub, key_slot = jax.random.split(key, 4)
    per_piece = PIECE // B
    seg_blocks = GRID_COLS * per_piece
    shape = (GRID_ROWS, GRID_COLS, TILES_DEV)
    grid_row = jnp.arange(GRID_ROWS, dtype=jnp.int32)[:, None, None]
    grid_col = jnp.arange(GRID_COLS, dtype=jnp.int32)[None, :, None]
    row_offset = jax.random.randint(key_row, shape, 0, seg_blocks, jnp.int32)
    tile_row = grid_row * seg_blocks + row_offset
    picks = jax.random.randint(key_piece, shape, 0, 1 << 20, jnp.int32)
    piece_row = picks % (grid_row + 1)
    sub_block = jax.random.randint(key_sub, shape, 0, per_piece, jnp.int32)
    tile_col = (piece_row * GRID_COLS + grid_col) * per_piece + sub_block
    tile_row = jnp.maximum(tile_row, tile_col)
    slot_keys = jax.random.split(key_slot, GRID_ROWS * GRID_COLS)
    slots = jax.vmap(lambda one_key: jax.random.permutation(one_key, TILES_DEV))(slot_keys)
    slots = slots.reshape(shape).astype(jnp.int32)
    return jnp.stack([tile_row, tile_col, slots], 0).astype(jnp.int32)


def draw_tile_count(key, part):
    key = jax.random.fold_in(key, 4)
    grid_row = jnp.arange(GRID_ROWS, dtype=jnp.int32)[:, None]
    base_count = (TILES_DEV * (grid_row + 1) + GRID_ROWS - 1) // GRID_ROWS
    reduction = jax.random.randint(key, (GRID_ROWS, GRID_COLS), 0, 3, jnp.int32)
    counts = jnp.maximum(base_count - reduction, 1)
    counts = jnp.where(grid_row == GRID_ROWS - 1, TILES_DEV, counts)
    return counts.astype(jnp.int32)


def shard_levels(own_key, dims, pieces, least, high):
    level = 1.0
    for axis_at, parts in pieces:
        heights = jax.random.uniform(jax.random.fold_in(jax.random.fold_in(own_key, 6), axis_at), (parts,), jnp.float32, least / len(pieces), high / len(pieces))
        level = level * jnp.repeat(jnp.exp(heights), dims[axis_at] // parts).reshape((-1,) + (1,) * (len(dims) - 1 - axis_at))
    return level


def scatter_about(own_key, shape, width, reach, shards=(), held_as=jnp.bfloat16):
    entries = width * jax.random.normal(own_key, shape, jnp.float32)
    if shards:
        entries = entries * shard_levels(own_key, shape, shards, -0.22, 0.18)
    return jnp.clip(entries, -reach, reach).astype(held_as)


def setup_inputs(seed: int = 0) -> dict:
    key_of = jax.random.split(jax.random.key(seed), 11)
    return {
        "tile_data": scatter_about(key_of[0], (GRID_ROWS, GRID_COLS, TILES_DEV, B, B), (B // 16) ** -0.5, 1.5, ((0, 32), (1, 16))),
        "tile_list": draw_tile_list(jax.random.fold_in(key_of[10], 71), 0),
        "tile_count": draw_tile_count(jax.random.fold_in(key_of[10], 71), 0),
        "current": draw_current(jax.random.fold_in(key_of[10], 71), 0),
        "current_image": draw_current_image(jax.random.fold_in(key_of[10], 71), 0),
        "direction": draw_direction(jax.random.fold_in(key_of[10], 71), 0),
        "direction_image": draw_direction_image(jax.random.fold_in(key_of[10], 71), 0),
        "energies": draw_energies(jax.random.fold_in(key_of[10], 71), 0),
        "precond": jnp.clip(jnp.exp(math.log(1.0) - 1.609438 * jax.random.uniform(key_of[8], (N,), jnp.float32) ** shard_levels(key_of[8], (N,), ((0, 512),), -0.2, 0.2)), 0.2, 1.0),
        "ritz_prev": jnp.clip(jax.random.uniform(key_of[9], (NVEC,), jnp.float32, 0.5, 3.5), 0.5, 3.5),
    }


def apply_tiles(tile_data, tile_list, tile_count, vectors):
    grid_rows = tile_data.shape[0]
    grid_cols = tile_data.shape[1]
    slots_dev = tile_data.shape[2]
    tile_width = tile_data.shape[3]
    flat_tiles = tile_data.reshape(grid_rows * grid_cols * slots_dev, tile_width, tile_width)
    offsets = (jnp.arange(grid_rows * grid_cols, dtype=jnp.int32) * slots_dev).reshape(grid_rows, grid_cols, 1)
    stored_at = (offsets + tile_list[2]).reshape(-1).astype(jnp.int32)
    tile_rows = tile_list[0].reshape(-1).astype(jnp.int32)
    tile_cols = tile_list[1].reshape(-1).astype(jnp.int32)
    positions = jnp.arange(slots_dev, dtype=jnp.int32)
    live_flags = (positions[None, None, :] < tile_count[:, :, None]).reshape(-1).astype(jnp.float32)

    def one_tile(totals, entry):
        slot_index, row_block, col_block, is_alive = entry
        tile_block = lax.dynamic_index_in_dim(flat_tiles, slot_index, 0, keepdims=False).astype(jnp.float32)
        row_start = row_block * tile_width
        col_start = col_block * tile_width
        source_col = lax.dynamic_slice_in_dim(vectors, col_start, tile_width, 1)
        source_row = lax.dynamic_slice_in_dim(vectors, row_start, tile_width, 1)
        direct_term = jnp.dot(source_col, tile_block.T, precision=lax.Precision.HIGHEST) * is_alive
        mirror_term = jnp.dot(source_row, tile_block, precision=lax.Precision.HIGHEST) * is_alive
        totals = lax.dynamic_update_slice_in_dim(totals, lax.dynamic_slice_in_dim(totals, row_start, tile_width, 1) + direct_term, row_start, 1)
        totals = lax.dynamic_update_slice_in_dim(totals, lax.dynamic_slice_in_dim(totals, col_start, tile_width, 1) + mirror_term, col_start, 1)
        return (totals, None)
    start_totals = jnp.zeros(vectors.shape, jnp.float32)
    totals, _ = lax.scan(one_tile, start_totals, (stored_at, tile_rows, tile_cols, live_flags))
    return totals

def project(gram_h, gram_s):
    symmetric = 0.5 * (gram_h + gram_h.T)
    lower = jnp.linalg.cholesky(gram_s)
    halfway = jax.scipy.linalg.solve_triangular(lower, symmetric, lower=True)
    whitened = jax.scipy.linalg.solve_triangular(lower, halfway.T, lower=True)
    return 0.5 * (whitened + whitened.T)

def reference(tile_data, tile_list, tile_count, current, current_image, direction, direction_image, energies, precond, ritz_prev):
    residual = precond[None, :] * (current_image - ritz_prev[:, None] * current)
    coupling = apply_tiles(tile_data, tile_list, tile_count, residual)
    applied = energies[None, :] * residual + coupling
    span_rows = jnp.concatenate([current, residual, direction], 0)
    image_rows = jnp.concatenate([current_image, applied, direction_image], 0)
    gram_h = jnp.dot(span_rows, image_rows.T, precision=lax.Precision.HIGHEST)
    gram_s = jnp.dot(span_rows, span_rows.T, precision=lax.Precision.HIGHEST)
    return (applied, project(gram_h, gram_s))
```

```python
import jax
import jax.numpy as jnp
from jax import lax
from jax.experimental import pallas as pl
from jax.experimental.pallas import tpu as pltpu
from jax.sharding import PartitionSpec as P

MESH = pl.DeviceIdType.MESH
HIGHEST = lax.Precision.HIGHEST
ZH, XN, YN = 4, 4, 8
NV, B, SUB, T = 8, 256, 8, 12
NT = (((1,), (1,)), ((), ()))
NN = (((1,), (0,)), ((), ()))
TN = (((0,), (0,)), ((), ()))

IDS = {}


def idx(*name):
    return IDS.setdefault(name, len(IDS))


def fill_ids():
    idx("zl")
    for way in (1, -1):
        for s in (1, 2, 3, 4):
            for p in (0, 1):
                idx("y", way, s, p)
                idx("ry", way, s, p)
        for d in range(ZH):
            idx("x", way, d)
            idx("xf", way, d)
            idx("rx2", way, d)
        idx("rx1", way)
    for d in range(1, ZH):
        idx("z", d)
        idx("rz", d)
    for e in range(XN):
        idx("rcore", e)
        for d in range(ZH):
            idx("core", e, d)
    idx("rzl")
    for stage in range(3):
        for d in range(1, 8):
            idx("ar", stage, d)


fill_ids()


def split3(v):
    hi = v.astype(jnp.bfloat16).astype(jnp.float32)
    rest = v - hi
    mid = rest.astype(jnp.bfloat16).astype(jnp.float32)
    low = rest - mid
    return jnp.concatenate([hi, mid, low], 0).astype(jnp.bfloat16)


def split_dot(v, tile, dims):
    out = lax.dot_general(split3(v), tile, dims, preferred_element_type=jnp.float32)
    return (out[16:24] + out[8:16]) + out[0:8]


def kernel(
    tile_hbm, list_s, count_s, cur, cimg, dirn, dimg, en, pre, ritz_s,
    applied, white,
    tiles, rbuf, cbuf, dbuf, mbuf, ry, rcore, rx1, rx2, rz, rzl, pd, pm, gram,
    table_v, table_s, prev_s, send, recv, local_sem,
):
    r = lax.axis_index("row")
    c = lax.axis_index("col")
    zh, x, co = r // 8, (r // 2) % 4, r % 2
    y, zl = c // 2, c % 2

    def dev(zh_, x_, co_, y_, zl_):
        return ((zh_ * 4 + x_) * 2 + co_, y_ * 2 + zl_)

    def at(dz=0, dx=0, dco=0, dy=0, dzl=0):
        return dev((zh + dz) % 4, (x + dx) % 4, (co + dco) % 2, (y + dy) % 8, (zl + dzl) % 2)

    def cx_peer(d):
        q = (x * 2 + co + d) % 8
        return dev(zh, q // 2, q % 2, y, zl)

    def z_peer(d):
        q = (zh * 2 + zl + d) % 8
        return dev(q // 2, x, co, y, q % 2)

    def y_peer(d):
        return dev(zh, x, co, (y + d) % 8, zl)

    tile_copy = pltpu.make_async_copy(tile_hbm.at[0, 0], tiles, local_sem.at[0])
    tile_copy.start()

    barrier = pltpu.get_barrier_semaphore()
    for d in range(1, 8):
        for peer in (cx_peer(d), z_peer(d), y_peer(d)):
            pl.semaphore_signal(barrier, inc=1, device_id=peer, device_id_type=MESH)

    copies = {}

    def go(name, src, dst, target):
        k = idx(*name)
        copy = pltpu.make_async_remote_copy(
            src_ref=src, dst_ref=dst, send_sem=send.at[k], recv_sem=recv.at[k],
            device_id=target, device_id_type=MESH,
        )
        copy.start()
        copies[name] = copy

    def got(*name):
        copies[name].wait_recv()

    rows = lax.broadcasted_iota(jnp.int32, (NV, B), 0)
    ritz = jnp.zeros((NV, B), jnp.float32)
    for a in range(NV):
        ritz = jnp.where(rows == a, ritz_s[a], ritz)
    for s in range(SUB):
        cols = slice(s * B, (s + 1) * B)
        piece = pre[:, cols] * (cimg[:, cols] - ritz * cur[:, cols])
        rbuf[c, s] = piece
        cbuf[co, x, zh, s] = piece

    pl.semaphore_wait(barrier, 21)

    def send_y(s, p, way):
        at_piece = rbuf.at[((y + way * (1 - s)) % 8) * 2 + (zl + p) % 2]
        go(("y", way, s, p), at_piece, at_piece, at(dy=way))

    def send_x(d):
        at_piece = cbuf.at[co, x, (zh - d) % 4]
        for way in (1, -1):
            go(("x", way, d), at_piece, at_piece, at(dx=way))

    def send_core(e, d):
        at_piece = cbuf.at[co, (x - e) % 4, (zh - d) % 4]
        go(("core", e, d), at_piece, at_piece, at(dco=1))

    def forward_x(d):
        way = 1 if d < 2 else -1
        at_piece = cbuf.at[co, (x - way) % 4, (zh - d) % 4]
        go(("xf", way, d), at_piece, at_piece, at(dx=way))

    def arrived_x(d):
        got("x", 1, d)
        got("x", -1, d)
        forward_x(d)
        send_core(1, d)
        send_core(3, d)

    def arrived_z(d):
        got("z", d)
        send_x(d)
        send_core(0, d)

    def arrived_y(s, p, ways=(1, -1)):
        for way in ways:
            got("y", way, s, p)
            send_y(s + 1, p, way)

    own = rbuf.at[c]
    go(("zl",), own, own, at(dzl=1))
    send_y(1, 0, 1)
    send_y(1, 0, -1)
    send_x(0)
    own_c = cbuf.at[co, x, zh]
    for d in (1, 3, 2):
        go(("z", d), own_c, own_c, at(dz=d))
    send_core(0, 0)

    lanes = lax.broadcasted_iota(jnp.int32, (1, 128), 1)
    live = count_s[0, 0]
    row_at = []
    col_at = []
    for k in range(T):
        i = list_s[0, 0, 0, k] & 127
        j = list_s[1, 0, 0, k]
        rr = j >> 7
        row_at.append(i)
        col_at.append((((rr & 1) * 4 + ((rr >> 1) & 3)) * 4 + (rr >> 3)) * 8 + (j & 7))
    tab = [jnp.full((1, 128), T, jnp.int32) for _ in range(3)]
    for k in range(T):
        row_live = jnp.where(k < live, row_at[k], -1)
        col_live = jnp.where(k < live, col_at[k], -1)
        tab[0] = jnp.where(lanes == row_live, k, tab[0])
        tab[1] = jnp.where(lanes == col_live, k, tab[1])
        tab[2] = jnp.where(lanes + 128 == col_live, k, tab[2])
        before_d = jnp.int32(T)
        before_m = jnp.int32(T)
        for q in range(k):
            before_d = jnp.where(row_at[q] == row_at[k], q, before_d)
            before_m = jnp.where(col_at[q] == col_at[k], q, before_m)
        prev_s[0, k] = before_d
        prev_s[1, k] = before_m
    table_v[...] = jnp.zeros_like(table_v)
    for q in range(3):
        table_v[q : q + 1, :] = tab[q]
    table_copy = pltpu.make_async_copy(table_v, table_s, local_sem.at[1])
    table_copy.start()
    pd[T] = jnp.zeros((NV, B), jnp.float32)
    pm[T] = jnp.zeros((NV, B), jnp.float32)

    got("zl")
    send_y(1, 1, 1)
    send_y(1, 1, -1)
    arrived_x(0)
    arrived_y(1, 0)
    arrived_z(1)
    arrived_y(1, 1)
    arrived_z(3)
    arrived_x(1)
    arrived_y(2, 0)
    arrived_z(2)
    arrived_y(2, 1)
    arrived_x(3)
    arrived_y(3, 0, (1,))
    got("y", -1, 3, 0)
    arrived_x(2)
    arrived_y(3, 1, (-1,))
    got("y", 1, 3, 1)
    for d in range(4):
        got("xf", 1 if d < 2 else -1, d)
        send_core(2, d)
    got("y", 1, 4, 0)
    got("y", -1, 4, 1)
    tile_copy.wait()
    table_copy.wait()
    for e in range(XN):
        for d in range(ZH):
            got("core", e, d)

    for k in range(T):
        i = list_s[0, 0, 0, k] & 127
        j = list_s[1, 0, 0, k]
        rr = j >> 7
        tile = tiles[list_s[2, 0, 0, k]]
        source_col = cbuf[rr & 1, (rr >> 1) & 3, rr >> 3, j & 7]
        source_row = rbuf[i >> 3, i & 7]
        pm[k] = split_dot(source_row, tile, NN) + pm[prev_s[1, k]]
        pd[k] = split_dot(source_col, tile, NT) + pd[prev_s[0, k]]

    def fill_m(half, xs):
        def step(q, carry):
            zq = q // 8
            sq = q % 8
            b = ((half * 4 + xs) * 4) * 8 + q
            mbuf[half, xs, zq, sq] = pm[table_s[1 + b // 128, b % 128]]
            return carry

        lax.fori_loop(0, 32, step, 0, unroll=8)

    def fill_d(q, carry):
        dbuf[q // 8, q % 8] = pd[table_s[0, q]]
        return carry

    def add(ref, *others):
        total = ref[...]
        for other in others:
            total = total + other[...]
        ref[...] = total

    for e in (2, 1, 3, 0):
        xs = (x + e) % 4
        fill_m(1 - co, xs)
        go(("rcore", e), mbuf.at[1 - co, xs], rcore.at[xs], at(dco=1))
    lax.fori_loop(0, 128, fill_d, 0, unroll=8)

    def dpiece(dy, p):
        return dbuf.at[((y + dy) % 8) * 2 + (zl + p) % 2]

    def send_ry(s, p, way):
        go(("ry", way, s, p), dpiece(way * (5 - s), p), ry.at[(1 - way) // 2, s - 1, p], at(dy=way))

    def arrived_ry(s, p, way):
        got("ry", way, s, p)
        add(dpiece(way * (4 - s), p), ry.at[(1 - way) // 2, s - 1, p])
        send_ry(s + 1, p, way)

    send_ry(1, 0, 1)
    send_ry(1, 1, -1)
    send_ry(2, 1, 1)
    send_ry(2, 0, -1)
    for e in (2, 1, 3, 0):
        fill_m(co, (x + e) % 4)

    def mpiece(dx, zq):
        return mbuf.at[co, (x + dx) % 4, zq]

    def arrived_core(e):
        got("rcore", e)
        xs = (x + e) % 4
        add(mbuf.at[co, xs], rcore.at[xs])

    arrived_core(2)
    for way in (1, -1):
        half = pl.ds(0 if way == 1 else 2, 2)
        go(("rx1", way), mbuf.at[co, (x + 2) % 4, half], rx1.at[(1 - way) // 2], at(dx=way))

    def send_rx2(zq, way):
        go(("rx2", way, zq), mpiece(way, zq), rx2.at[(1 - way) // 2, zq], at(dx=way))

    arrived_ry(1, 0, 1)
    arrived_ry(1, 1, -1)
    arrived_core(1)
    arrived_core(3)
    send_rx2(2, 1)
    send_rx2(0, -1)
    send_rx2(3, 1)
    send_rx2(1, -1)
    arrived_ry(2, 1, 1)
    arrived_ry(2, 0, -1)
    arrived_core(0)
    got("rx1", 1)
    got("rx1", -1)
    for q in range(2):
        add(mpiece(1, q), rx1.at[0, q])
        send_rx2(q, 1)
        add(mpiece(-1, 2 + q), rx1.at[1, q])
        send_rx2(2 + q, -1)
    arrived_ry(2, 0, 1)
    arrived_ry(2, 1, -1)
    arrived_ry(3, 1, 1)
    arrived_ry(3, 0, -1)

    def arrived_rx2(zq):
        got("rx2", 1, zq)
        got("rx2", -1, zq)
        add(mpiece(0, zq), rx2.at[0, zq], rx2.at[1, zq])

    for zq in range(4):
        arrived_rx2(zq)
    for d in (2, 1, 3):
        go(("rz", d), mbuf.at[co, x, (zh + d) % 4], rz.at[d - 1], at(dz=d))
    arrived_ry(3, 0, 1)
    arrived_ry(3, 1, -1)
    for p in (1, 0):
        got("ry", 1, 4, p)
        got("ry", -1, 4, p)
        add(dpiece(0, p), ry.at[0, 3, p], ry.at[1, 3, p])
        if p == 1:
            go(("rzl",), dpiece(0, 1), rzl, at(dzl=1))
    for d in (1, 3, 2):
        got("rz", d)
    got("rzl")

    for s in range(SUB):
        cols = slice(s * B, (s + 1) * B)
        direct = dbuf[c, s] + rzl[s]
        mirror = (mbuf[co, x, zh, s] + rz[0, s]) + (rz[1, s] + rz[2, s])
        applied[:, cols] = en[:, cols] * rbuf[c, s] + (direct + mirror)

    residual = jnp.concatenate([rbuf[c, s] for s in range(SUB)], 1)
    span = jnp.concatenate([cur[...], residual, dirn[...]], 0)
    images = jnp.concatenate([cimg[...], applied[...], dimg[...]], 0)
    gram[0, 0] = jnp.zeros_like(gram[0, 0])
    gram[0, 0, 0, :, 0:24] = lax.dot_general(span, images, NT, precision=HIGHEST, preferred_element_type=jnp.float32)
    gram[0, 0, 1, :, 0:24] = lax.dot_general(span, span, NT, precision=HIGHEST, preferred_element_type=jnp.float32)
    total = gram[0, 0]
    for stage, peer, me in ((0, cx_peer, x * 2 + co), (1, z_peer, zh * 2 + zl), (2, y_peer, y)):
        gram[1 + stage, me] = total
        for d in range(1, 8):
            mine = gram.at[1 + stage, me]
            go(("ar", stage, d), mine, mine, peer(d))
        for d in range(1, 8):
            got("ar", stage, d)
        total = gram[1 + stage, 0]
        for q in range(1, 8):
            total = total + gram[1 + stage, q]

    gram_h = total[0, :, 0:24]
    gram_s = total[1, :, 0:24]
    at_row = lax.broadcasted_iota(jnp.int32, (24, 24), 0)
    at_col = lax.broadcasted_iota(jnp.int32, (24, 24), 1)
    eye = jnp.where(at_row == at_col, 1.0, 0.0).astype(jnp.float32)
    left, inverse = gram_s, eye
    for k in range(24):
        root = jnp.sqrt(left[k : k + 1, k : k + 1])
        row = left[k : k + 1, :] / root
        row_inverse = inverse[k : k + 1, :] / root
        factor = left[:, k : k + 1] / root
        left = jnp.where(at_row > k, left - factor * row, jnp.where(at_row == k, row, left))
        inverse = jnp.where(
            at_row > k, inverse - factor * row_inverse, jnp.where(at_row == k, row_inverse, inverse)
        )

    def dot(a, b, dims):
        return lax.dot_general(a, b, dims, precision=HIGHEST, preferred_element_type=jnp.float32)

    symmetric = 0.5 * (gram_h + dot(gram_h, eye, TN))
    white[...] = dot(dot(inverse, symmetric, NN), inverse, NT)

    for copy in copies.values():
        copy.wait_send()


def body(
    tile_data, tile_list, tile_count, current, current_image, direction, direction_image,
    energies, precond, ritz_prev,
):
    vmem = pl.BlockSpec(memory_space=pltpu.VMEM)
    smem = pl.BlockSpec(memory_space=pltpu.SMEM)
    f32 = jnp.float32
    n_ids = len(IDS)
    applied, white = pl.pallas_call(
        kernel,
        out_shape=(jax.ShapeDtypeStruct(current.shape, f32), jax.ShapeDtypeStruct((24, 24), f32)),
        in_specs=[pl.BlockSpec(memory_space=pl.ANY), smem, smem, vmem, vmem, vmem, vmem, vmem, vmem, smem],
        out_specs=(vmem, vmem),
        scratch_shapes=[
            pltpu.VMEM((T, B, B), jnp.bfloat16),
            pltpu.VMEM((16, SUB, NV, B), f32),
            pltpu.VMEM((2, XN, ZH, SUB, NV, B), f32),
            pltpu.VMEM((16, SUB, NV, B), f32),
            pltpu.VMEM((2, XN, ZH, SUB, NV, B), f32),
            pltpu.VMEM((2, 4, 2, SUB, NV, B), f32),
            pltpu.VMEM((XN, ZH, SUB, NV, B), f32),
            pltpu.VMEM((2, 2, SUB, NV, B), f32),
            pltpu.VMEM((2, ZH, SUB, NV, B), f32),
            pltpu.VMEM((3, SUB, NV, B), f32),
            pltpu.VMEM((SUB, NV, B), f32),
            pltpu.VMEM((T + 1, NV, B), f32),
            pltpu.VMEM((T + 1, NV, B), f32),
            pltpu.VMEM((4, 8, 2, 24, 128), f32),
            pltpu.VMEM((8, 128), jnp.int32),
            pltpu.SMEM((8, 128), jnp.int32),
            pltpu.SMEM((2, T), jnp.int32),
            pltpu.SemaphoreType.DMA((n_ids,)),
            pltpu.SemaphoreType.DMA((n_ids,)),
            pltpu.SemaphoreType.DMA((2,)),
        ],
        compiler_params=pltpu.CompilerParams(
            collective_id=0, has_side_effects=True, vmem_limit_bytes=40 * 1024 * 1024
        ),
        name="lobpcg_step",
    )(
        tile_data, tile_list, tile_count, current, current_image, direction, direction_image,
        energies.reshape(1, -1), precond.reshape(1, -1), ritz_prev,
    )
    return (applied, 0.5 * (white + white.T))


def solution(mesh):
    in_specs = (
        P("row", "col", None, None, None),
        P(None, "row", "col", None),
        P("row", "col"),
        P(None, ("row", "col")),
        P(None, ("row", "col")),
        P(None, ("row", "col")),
        P(None, ("row", "col")),
        P(("row", "col")),
        P(("row", "col")),
        P(),
    )
    out_specs = (P(None, ("row", "col")), P())
    return jax.shard_map(body, mesh=mesh, in_specs=in_specs, out_specs=out_specs, check_vma=False)
```

```python
import jax
import jax.numpy as jnp
from jax import lax
from jax.experimental import pallas as pl
from jax.experimental.pallas import tpu as pltpu
from jax.sharding import PartitionSpec as P

MESH = pl.DeviceIdType.MESH
HIGHEST = lax.Precision.HIGHEST
ZH, XN, YN = 4, 4, 8
NV, B, SUB, T = 8, 256, 8, 12
NT = (((1,), (1,)), ((), ()))
NN = (((1,), (0,)), ((), ()))
TN = (((0,), (0,)), ((), ()))

IDS = {}


def idx(*name):
    return IDS.setdefault(name, len(IDS))


def fill_ids():
    idx("zl")
    idx("rzl")
    idx("spl")
    for way in (1, -1):
        for p in (0, 1):
            for step in ("y1", "y2", "y3"):
                idx(step, way, p)
        idx("y4", way)
        for step in ("r1", "r2", "r3", "r4"):
            idx(step, way)
    for d in range(1, ZH):
        idx("z", d)
        idx("rz", d)
        idx("spz", d)
    for e in range(XN):
        idx("rcore", e)
        idx("rx", e)
        for g in range(3):
            idx("x", g, e)
            idx("core", g, e)
    for stage in range(3):
        for d in range(1, 8):
            idx("early", stage, d)
            idx("late", stage, d)


fill_ids()


def split3(v):
    hi = v.astype(jnp.bfloat16).astype(jnp.float32)
    rest = v - hi
    mid = rest.astype(jnp.bfloat16).astype(jnp.float32)
    low = rest - mid
    return jnp.concatenate([hi, mid, low], 0).astype(jnp.bfloat16)


def split_dot(v, tile, dims):
    out = lax.dot_general(split3(v), tile, dims, preferred_element_type=jnp.float32)
    return (out[16:24] + out[8:16]) + out[0:8]


def dot(a, b, dims):
    return lax.dot_general(a, b, dims, precision=HIGHEST, preferred_element_type=jnp.float32)


def cat(ref):
    return jnp.concatenate([ref[s] for s in range(SUB)], 1)


def kernel(
    tile_hbm, list_hbm, count_hbm, cur_hbm, cimg_hbm, dirn_hbm, dimg_hbm, en_hbm, pre_hbm, ritz_hbm,
    applied_hbm, white,
    list_s, count_s, own_cd, cimg, dimg, en, pre, ritz_s, tiles, rbuf, cbuf, dbuf, mbuf,
    ry1, ry2, ry3, ry4, rcore, rx, rz, rzl, spz, spl, pd, pm, early, late, applied,
    table_v, table_s, prev_s, send, recv, local_sem,
):
    r = lax.axis_index("row")
    c = lax.axis_index("col")
    zh, x, co = r // 8, (r // 2) % 4, r % 2
    y, zl = c // 2, c % 2

    def dev(zh_, x_, co_, y_, zl_):
        return ((zh_ * 4 + x_) * 2 + co_, y_ * 2 + zl_)

    def at(dz=0, dx=0, dco=0, dy=0, dzl=0):
        return dev((zh + dz) % 4, (x + dx) % 4, (co + dco) % 2, (y + dy) % 8, (zl + dzl) % 2)

    def cx_peer(d):
        q = (x * 2 + co + d) % 8
        return dev(zh, q // 2, q % 2, y, zl)

    def z_peer(d):
        q = (zh * 2 + zl + d) % 8
        return dev(q // 2, x, co, y, q % 2)

    def y_peer(d):
        return dev(zh, x, co, (y + d) % 8, zl)

    barrier = pltpu.get_barrier_semaphore()
    for d in range(1, 8):
        for peer in (cx_peer(d), z_peer(d), y_peer(d)):
            pl.semaphore_signal(barrier, inc=1, device_id=peer, device_id_type=MESH)

    local = {}
    for q, (name, src, dst) in enumerate((
        ("ritz", ritz_hbm, ritz_s), ("cimg", cimg_hbm, cimg), ("cur", cur_hbm, own_cd.at[0:8]), ("pre", pre_hbm, pre),
        ("list", list_hbm, list_s), ("count", count_hbm, count_s), ("dirn", dirn_hbm, own_cd.at[8:16]),
        ("dimg", dimg_hbm, dimg), ("en", en_hbm, en), ("tiles", tile_hbm.at[0, 0], tiles),
    )):
        local[name] = pltpu.make_async_copy(src, dst, local_sem.at[2 + q])
        local[name].start()

    copies = {}

    def go(name, src, dst, target):
        k = idx(*name)
        copy = pltpu.make_async_remote_copy(
            src_ref=src, dst_ref=dst, send_sem=send.at[k], recv_sem=recv.at[k],
            device_id=target, device_id_type=MESH,
        )
        copy.start()
        copies[name] = copy

    def got(*name):
        copies[name].wait_recv()

    for name in ("ritz", "cimg", "cur", "pre"):
        local.pop(name).wait()
    rows = lax.broadcasted_iota(jnp.int32, (NV, B), 0)
    ritz = jnp.zeros((NV, B), jnp.float32)
    for a in range(NV):
        ritz = jnp.where(rows == a, ritz_s[a], ritz)
    for s in range(SUB):
        cols = slice(s * B, (s + 1) * B)
        piece = pre[:, cols] * (cimg[:, cols] - ritz * own_cd[0:8, cols])
        rbuf[c, s] = piece
        cbuf[co, x, 0, s] = piece

    pl.semaphore_wait(barrier, 21)

    pos = (0, 1, 3, 2)
    group = (pl.ds(0, 1), pl.ds(1, 2), pl.ds(3, 1))

    def rpiece(dy, p):
        return rbuf.at[((y + dy) % 8) * 2 + (zl + p) % 2]

    def send_y(p):
        for step, hops in (("y2", 2), ("y1", 1)):
            for way in (1, -1):
                go((step, way, p), rpiece(0, p), rpiece(0, p), at(dy=hops * way))

    def arrived_y2(p):
        for way in (1, -1):
            got("y2", way, p)
            piece = rpiece(-2 * way, p)
            if p == (1 - way) // 2:
                go(("y4", way), piece, piece, at(dy=2 * way))
            go(("y3", way, p), piece, piece, at(dy=way))

    def send_core(g, e):
        part = cbuf.at[co, (x - e) % 4, group[g]]
        go(("core", g, e), part, part, at(dco=1))

    def send_x(g):
        part = cbuf.at[co, x, group[g]]
        for e in (2, 1, 3):
            go(("x", g, e), part, part, at(dx=e))
        send_core(g, 0)

    def arrived_x(g):
        for e in (1, 3, 2):
            got("x", g, e)
            send_core(g, e)

    own = rpiece(0, 0)
    own_c = cbuf.at[co, x, 0]
    go(("zl",), own, own, at(dzl=1))
    send_y(0)
    for d in (1, 3, 2):
        go(("z", d), own_c, cbuf.at[co, x, pos[d]], at(dz=d))
    send_x(0)

    local.pop("list").wait()
    local.pop("count").wait()
    lanes = lax.broadcasted_iota(jnp.int32, (1, 128), 1)
    live = count_s[0, 0]

    def row_block(k):
        return list_s[0, 0, 0, k] & 127

    def col_block(k):
        j = list_s[1, 0, 0, k]
        owner = j >> 7
        d = (zh - (owner >> 3)) & 3
        return owner & 1, (owner >> 1) & 3, d ^ (d >> 1), j & 7

    row_at = []
    col_at = []
    for k in range(T):
        row_at.append(row_block(k))
        core_k, x_k, pos_k, sub_k = col_block(k)
        col_at.append(((core_k * 4 + x_k) * 4 + pos_k) * 8 + sub_k)
    tab = [jnp.full((1, 128), T, jnp.int32) for _ in range(3)]
    for k in range(T):
        row_live = jnp.where(k < live, row_at[k], -1)
        col_live = jnp.where(k < live, col_at[k], -1)
        tab[0] = jnp.where(lanes == row_live, k, tab[0])
        tab[1] = jnp.where(lanes == col_live, k, tab[1])
        tab[2] = jnp.where(lanes + 128 == col_live, k, tab[2])
        before_d = jnp.int32(T)
        before_m = jnp.int32(T)
        for q in range(k):
            before_d = jnp.where(row_at[q] == row_at[k], q, before_d)
            before_m = jnp.where(col_at[q] == col_at[k], q, before_m)
        prev_s[0, k] = before_d
        prev_s[1, k] = before_m
    table_v[...] = jnp.zeros_like(table_v)
    for q in range(3):
        table_v[q : q + 1, :] = tab[q]
    local["table"] = pltpu.make_async_copy(table_v, table_s, local_sem.at[1])
    local["table"].start()
    pd[T] = jnp.zeros((NV, B), jnp.float32)
    pm[T] = jnp.zeros((NV, B), jnp.float32)

    got("zl")
    send_y(1)

    stages = ((cx_peer, x * 2 + co), (z_peer, zh * 2 + zl), (y_peer, y))

    def share(name, buf, stage, value):
        peer, me = stages[stage]
        buf[stage, me] = value
        for d in (4, 3, 5, 2, 6, 1, 7):
            go((name, stage, d), buf.at[stage, me], buf.at[stage, me], peer(d))

    def shared(name, buf, stage):
        for d in (4, 3, 5, 2, 6, 1, 7):
            got(name, stage, d)
        total = buf[stage, 0]
        for q in range(1, 8):
            total = total + buf[stage, q]
        return total

    for name in ("dirn", "dimg"):
        local.pop(name).wait()
    residual = cat(rbuf.at[c])
    span = jnp.concatenate([own_cd[0:8, :], residual, own_cd[8:16, :]], 0)
    known = jnp.concatenate([cimg[...], jnp.zeros_like(residual), dimg[...], span], 0)
    first = jnp.concatenate([dot(span, known, NT), jnp.zeros((24, 80), jnp.float32)], 1)
    share("early", early, 0, first)

    arrived_x(0)
    arrived_y2(0)
    got("z", 1)
    got("z", 3)
    send_x(1)
    got("z", 2)
    send_x(2)
    arrived_y2(1)
    for d in (2, 1, 3):
        go(("spz", d), own_cd, spz.at[d - 1], at(dz=d))
    go(("spl",), own_cd, spl, at(dzl=1))
    arrived_x(1)
    share("early", early, 1, shared("early", early, 0))
    for way in (1, -1):
        for p in (0, 1):
            got("y1", way, p)
            got("y3", way, p)
        got("y4", way)
    arrived_x(2)
    local.pop("tiles").wait()
    local.pop("table").wait()
    for g in range(3):
        for e in range(XN):
            got("core", g, e)

    for k in range(T):
        i = row_block(k)
        tile = tiles[list_s[2, 0, 0, k]]
        source_col = cbuf[col_block(k)]
        source_row = rbuf[i >> 3, i & 7]
        pd[k] = split_dot(source_col, tile, NT) + pd[prev_s[0, k]]
        pm[k] = split_dot(source_row, tile, NN) + pm[prev_s[1, k]]

    def fill_m(half, xs):
        def step(q, carry):
            b = ((half * 4 + xs) * 4) * 8 + q
            mbuf[half, xs, q // 8, q % 8] = pm[table_s[1 + b // 128, b % 128]]
            return carry

        lax.fori_loop(0, 32, step, 0, unroll=8)

    def fill_d(q, carry):
        dbuf[q // 8, q % 8] = pd[table_s[0, q]]
        return carry

    def add(ref, *others):
        total = ref[...]
        for other in others:
            total = total + other[...]
        ref[...] = total

    def dpair(dy):
        return dbuf.at[pl.ds(((y + dy) % 8) * 2, 2)]

    lax.fori_loop(0, 128, fill_d, 0, unroll=8)
    for way in (1, -1):
        w = (1 - way) // 2
        go(("r3", way), dpair(3 * way), ry3.at[w], at(dy=way))
        go(("r4", way), dbuf.at[((y + 4) % 8) * 2 + (zl + w) % 2], ry4.at[w], at(dy=2 * way))
    for e in (2, 1, 3, 0):
        xs = (x + e) % 4
        fill_m(1 - co, xs)
        go(("rcore", e), mbuf.at[1 - co, xs], rcore.at[xs], at(dco=1))
    for way in (1, -1):
        go(("r1", way), dpair(way), ry1.at[(1 - way) // 2], at(dy=way))
    for e in (2, 1, 3, 0):
        xs = (x + e) % 4
        fill_m(co, xs)
        got("rcore", e)
        add(mbuf.at[co, xs], rcore.at[xs])
        if e:
            go(("rx", e), mbuf.at[co, xs], rx.at[e - 1], at(dx=e))
    share("early", early, 2, shared("early", early, 1))

    for way in (1, -1):
        w = (1 - way) // 2
        got("r3", way)
        got("r4", way)
        add(dpair(2 * way), ry3.at[w])
        add(dbuf.at[((y + 2 * way) % 8) * 2 + (zl + w) % 2], ry4.at[w])
        go(("r2", way), dpair(2 * way), ry2.at[w], at(dy=2 * way))

    total = shared("early", early, 2)
    at_row = lax.broadcasted_iota(jnp.int32, (24, 24), 0)
    at_col = lax.broadcasted_iota(jnp.int32, (24, 24), 1)
    eye = jnp.where(at_row == at_col, 1.0, 0.0).astype(jnp.float32)
    left, inverse = total[:, 24:48], eye
    for k in range(24):
        root = jnp.sqrt(left[k : k + 1, k : k + 1])
        row = left[k : k + 1, :] / root
        row_inverse = inverse[k : k + 1, :] / root
        factor = left[:, k : k + 1] / root
        left = jnp.where(at_row > k, left - factor * row, jnp.where(at_row == k, row, left))
        inverse = jnp.where(
            at_row > k, inverse - factor * row_inverse, jnp.where(at_row == k, row_inverse, inverse)
        )
    white_known = dot(dot(inverse, total[:, 0:24], NN), inverse, NT)

    for d in (1, 2, 3):
        got("spz", d)
    got("spl")
    for e in (1, 2, 3):
        got("rx", e)
    add(mbuf.at[co, x], rx.at[0], rx.at[1], rx.at[2])
    for d in (2, 1, 3):
        go(("rz", d), mbuf.at[co, x, pos[d]], rz.at[d - 1], at(dz=-d))
    for step in ("r1", "r2"):
        for way in (1, -1):
            got(step, way)
    add(dpair(0), ry1.at[0], ry1.at[1], ry2.at[0], ry2.at[1])
    other_c = y * 2 + (1 - zl)
    go(("rzl",), dbuf.at[other_c], rzl, at(dzl=1))

    local.pop("en").wait()
    for s in range(SUB):
        cols = slice(s * B, (s + 1) * B)
        applied[:, cols] = en[:, cols] * rbuf[c, s] + (dbuf[c, s] + mbuf[co, x, 0, s])

    def partial_gram(image, own_span, res):
        return dot(image, jnp.concatenate([own_span[0:8, :], res, own_span[8:16, :]], 0), NT)

    gram = partial_gram(applied[...], own_cd, cat(rbuf.at[c]))
    gram = gram + partial_gram(cat(dbuf.at[other_c]), spl, cat(rbuf.at[other_c]))
    for d in (1, 2, 3):
        gram = gram + partial_gram(cat(mbuf.at[co, x, pos[d]]), spz.at[d - 1], cat(cbuf.at[co, x, pos[d]]))
    gram = jnp.concatenate([gram, jnp.zeros((NV, 104), jnp.float32)], 1)

    share("late", late, 0, gram)
    share("late", late, 2, shared("late", late, 0))
    gram = shared("late", late, 2)
    share("late", late, 1, gram)

    for d in (1, 3, 2):
        got("rz", d)
    got("rzl")
    for s in range(SUB):
        cols = slice(s * B, (s + 1) * B)
        applied[:, cols] = applied[:, cols] + (rzl[s] + (rz[0, s] + rz[1, s] + rz[2, s]))
    local["applied"] = pltpu.make_async_copy(applied, applied_hbm, local_sem.at[0])
    local["applied"].start()
    gram = shared("late", late, 1)[:, 0:24]

    white_all = white_known + dot(inverse[:, 8:16], dot(gram, inverse, NT), NN)
    whitened = 0.5 * (white_all + dot(white_all, eye, TN))
    white[...] = 0.5 * (whitened + dot(whitened, eye, TN))
    local.pop("applied").wait()

    for copy in copies.values():
        copy.wait_send()


def body(
    tile_data, tile_list, tile_count, current, current_image, direction, direction_image,
    energies, precond, ritz_prev,
):
    vmem = pl.BlockSpec(memory_space=pltpu.VMEM)
    hbm = pl.BlockSpec(memory_space=pltpu.HBM)
    f32 = jnp.float32
    n_ids = len(IDS)
    applied, white = pl.pallas_call(
        kernel,
        out_shape=(jax.ShapeDtypeStruct(current.shape, f32), jax.ShapeDtypeStruct((24, 24), f32)),
        in_specs=[hbm] * 10,
        out_specs=(hbm, vmem),
        scratch_shapes=[
            pltpu.SMEM(tile_list.shape, jnp.int32),
            pltpu.SMEM((1, 1), jnp.int32),
            pltpu.VMEM((2 * NV, SUB * B), f32),
            pltpu.VMEM(current.shape, f32),
            pltpu.VMEM(current.shape, f32),
            pltpu.VMEM((1, SUB * B), f32),
            pltpu.VMEM((1, SUB * B), f32),
            pltpu.SMEM((NV,), f32),
            pltpu.VMEM((T, B, B), jnp.bfloat16),
            pltpu.VMEM((16, SUB, NV, B), f32),
            pltpu.VMEM((2, XN, ZH, SUB, NV, B), f32),
            pltpu.VMEM((16, SUB, NV, B), f32),
            pltpu.VMEM((2, XN, ZH, SUB, NV, B), f32),
            pltpu.VMEM((2, 2, SUB, NV, B), f32),
            pltpu.VMEM((2, 2, SUB, NV, B), f32),
            pltpu.VMEM((2, 2, SUB, NV, B), f32),
            pltpu.VMEM((2, SUB, NV, B), f32),
            pltpu.VMEM((XN, ZH, SUB, NV, B), f32),
            pltpu.VMEM((3, ZH, SUB, NV, B), f32),
            pltpu.VMEM((3, SUB, NV, B), f32),
            pltpu.VMEM((SUB, NV, B), f32),
            pltpu.VMEM((3, 2 * NV, SUB * B), f32),
            pltpu.VMEM((2 * NV, SUB * B), f32),
            pltpu.VMEM((T + 1, NV, B), f32),
            pltpu.VMEM((T + 1, NV, B), f32),
            pltpu.VMEM((3, 8, 24, 128), f32),
            pltpu.VMEM((3, 8, NV, 128), f32),
            pltpu.VMEM(current.shape, f32),
            pltpu.VMEM((8, 128), jnp.int32),
            pltpu.SMEM((8, 128), jnp.int32),
            pltpu.SMEM((2, T), jnp.int32),
            pltpu.SemaphoreType.DMA((n_ids,)),
            pltpu.SemaphoreType.DMA((n_ids,)),
            pltpu.SemaphoreType.DMA((12,)),
        ],
        compiler_params=pltpu.CompilerParams(
            collective_id=0, has_side_effects=True, vmem_limit_bytes=60 * 1024 * 1024
        ),
        name="lobpcg_step",
    )(
        tile_data, tile_list, tile_count, current, current_image, direction, direction_image,
        energies.reshape(1, -1), precond.reshape(1, -1), ritz_prev,
    )
    return (applied, white)


def solution(mesh):
    in_specs = (
        P("row", "col", None, None, None),
        P(None, "row", "col", None),
        P("row", "col"),
        P(None, ("row", "col")),
        P(None, ("row", "col")),
        P(None, ("row", "col")),
        P(None, ("row", "col")),
        P(("row", "col")),
        P(("row", "col")),
        P(),
    )
    out_specs = (P(None, ("row", "col")), P())
    return jax.shard_map(body, mesh=mesh, in_specs=in_specs, out_specs=out_specs, check_vma=False)
```

```python
import jax
import jax.numpy as jnp
from jax import lax
from jax.experimental import pallas as pl
from jax.experimental.pallas import tpu as pltpu
from jax.sharding import PartitionSpec as P

MESH = pl.DeviceIdType.MESH
HIGHEST = lax.Precision.HIGHEST
ZH, XN, YN = 4, 4, 8
NV, B, SUB, T = 8, 256, 8, 12
NT = (((1,), (1,)), ((), ()))
NN = (((1,), (0,)), ((), ()))
TN = (((0,), (0,)), ((), ()))

IDS = {}


def idx(*name):
    return IDS.setdefault(name, len(IDS))


def fill_ids():
    idx("zl")
    idx("rzl")
    idx("spl")
    for way in (1, -1):
        for p in (0, 1):
            for step in ("y1", "y2", "y3"):
                idx(step, way, p)
        idx("y4", way)
        for step in ("r1", "r2", "r3", "r4"):
            idx(step, way)
    for d in (1, 3):
        idx("zf", d)
        idx("zx", d)
    idx("rx2", 0)
    idx("rx2", 3)
    for d in range(1, ZH):
        idx("z", d)
        idx("rz", d)
        idx("spz", d)
    for e in range(XN):
        idx("rcore", e)
        idx("rx", e)
        for g in range(4):
            idx("x", g, e)
            idx("core", g, e)
    for stage in range(3):
        for d in range(1, 8):
            idx("early", stage, d)
            idx("late", stage, d)


fill_ids()


def split3(v):
    hi = v.astype(jnp.bfloat16).astype(jnp.float32)
    rest = v - hi
    mid = rest.astype(jnp.bfloat16).astype(jnp.float32)
    low = rest - mid
    return jnp.concatenate([hi, mid, low], 0).astype(jnp.bfloat16)


def split_dot(v, tile, dims):
    out = lax.dot_general(split3(v), tile, dims, preferred_element_type=jnp.float32)
    return (out[16:24] + out[8:16]) + out[0:8]


def dot(a, b, dims):
    return lax.dot_general(a, b, dims, precision=HIGHEST, preferred_element_type=jnp.float32)


def cat(ref):
    return jnp.concatenate([ref[s] for s in range(SUB)], 1)


def kernel(
    tile_hbm, list_hbm, count_hbm, cur_hbm, cimg_hbm, dirn_hbm, dimg_hbm, en_hbm, pre_hbm, ritz_hbm,
    applied, white,
    list_s, count_s, own_cd, cimg, dimg, en, pre, ritz_s, tiles, rbuf, cbuf, dbuf, mbuf,
    ry1, ry2, ry3, ry4, rcore, rx, rx2, zx, rz, rzl, spz, spl, pd, pm, early, late,
    table_v, table_s, prev_s, send, recv, local_sem,
):
    r = lax.axis_index("row")
    c = lax.axis_index("col")
    zh, x, co = r // 8, (r // 2) % 4, r % 2
    y, zl = c // 2, c % 2

    def dev(zh_, x_, co_, y_, zl_):
        return ((zh_ * 4 + x_) * 2 + co_, y_ * 2 + zl_)

    def at(dz=0, dx=0, dco=0, dy=0, dzl=0):
        return dev((zh + dz) % 4, (x + dx) % 4, (co + dco) % 2, (y + dy) % 8, (zl + dzl) % 2)

    def cx_peer(d):
        q = (x * 2 + co + d) % 8
        return dev(zh, q // 2, q % 2, y, zl)

    def z_peer(d):
        q = (zh * 2 + zl + d) % 8
        return dev(q // 2, x, co, y, q % 2)

    def y_peer(d):
        return dev(zh, x, co, (y + d) % 8, zl)

    barrier = pltpu.get_barrier_semaphore()
    near = [at(dz=1), at(dz=3), at(dy=2), at(dy=6), at(dx=2), at(dzl=1), at(dy=1), at(dy=7), at(dx=1), at(dx=3), at(dco=1)]
    for peer in near:
        pl.semaphore_signal(barrier, inc=1, device_id=peer, device_id_type=MESH)

    local = {}
    for q, (name, src, dst) in enumerate((
        ("ritz", ritz_hbm, ritz_s), ("cimg", cimg_hbm, cimg), ("cur", cur_hbm, own_cd.at[0:8]), ("pre", pre_hbm, pre),
        ("list", list_hbm, list_s), ("count", count_hbm, count_s), ("dirn", dirn_hbm, own_cd.at[8:16]),
        ("dimg", dimg_hbm, dimg), ("en", en_hbm, en), ("tiles", tile_hbm.at[0, 0], tiles),
    )):
        local[name] = pltpu.make_async_copy(src, dst, local_sem.at[2 + q])
        local[name].start()

    copies = {}

    def go(name, src, dst, target):
        k = idx(*name)
        copy = pltpu.make_async_remote_copy(
            src_ref=src, dst_ref=dst, send_sem=send.at[k], recv_sem=recv.at[k],
            device_id=target, device_id_type=MESH,
        )
        copy.start()
        copies[name] = copy

    def got(*name):
        copies[name].wait_recv()

    for name in ("ritz", "cimg", "cur", "pre"):
        local.pop(name).wait()
    rows = lax.broadcasted_iota(jnp.int32, (NV, B), 0)
    ritz = jnp.zeros((NV, B), jnp.float32)
    for a in range(NV):
        ritz = jnp.where(rows == a, ritz_s[a], ritz)
    for s in range(SUB):
        cols = slice(s * B, (s + 1) * B)
        piece = pre[:, cols] * (cimg[:, cols] - ritz * own_cd[0:8, cols])
        rbuf[c, s] = piece
        cbuf[co, x, 0, s] = piece

    pl.semaphore_wait(barrier, len(near))

    pos = (0, 1, 3, 2)
    whole = pl.ds(0, 8)
    group = ((pl.ds(0, 1), whole), (pl.ds(1, 2), whole), (pl.ds(3, 1), pl.ds(0, 4)), (pl.ds(3, 1), pl.ds(4, 4)))

    def rpiece(dy, p):
        return rbuf.at[((y + dy) % 8) * 2 + (zl + p) % 2]

    def send_y(p):
        for step, hops in (("y2", 2), ("y1", 1)):
            for way in (1, -1):
                go((step, way, p), rpiece(0, p), rpiece(0, p), at(dy=hops * way))

    def arrived_y2(p):
        for way in (1, -1):
            got("y2", way, p)
            piece = rpiece(-2 * way, p)
            if p == (1 - way) // 2:
                go(("y4", way), piece, piece, at(dy=2 * way))
            go(("y3", way, p), piece, piece, at(dy=way))

    def send_core(g, e):
        part = cbuf.at[(co, (x - e) % 4) + group[g]]
        go(("core", g, e), part, part, at(dco=1))

    def send_x(g):
        part = cbuf.at[(co, x) + group[g]]
        for e in (2, 1, 3):
            go(("x", g, e), part, part, at(dx=e))
        send_core(g, 0)

    def arrived_x(g):
        for e in (1, 3, 2):
            got("x", g, e)
            send_core(g, e)

    own = rpiece(0, 0)
    own_c = cbuf.at[co, x, 0]
    go(("zl",), own, own, at(dzl=1))
    for d in (1, 3):
        go(("z", d), own_c, cbuf.at[co, x, pos[d]], at(dz=d))
    send_y(0)
    send_x(0)

    def arrived_z():
        for d in (1, 3):
            got("z", d)
            half = pl.ds(0 if d == 1 else 4, 4)
            go(("zf", d), cbuf.at[co, x, pos[d], half], cbuf.at[co, x, 3, half], at(dz=d))
        send_x(1)

    local.pop("list").wait()
    local.pop("count").wait()
    lanes = lax.broadcasted_iota(jnp.int32, (1, 128), 1)
    live = count_s[0, 0]

    def row_block(k):
        return list_s[0, 0, 0, k] & 127

    def col_block(k):
        j = list_s[1, 0, 0, k]
        owner = j >> 7
        d = (zh - (owner >> 3)) & 3
        return owner & 1, (owner >> 1) & 3, d ^ (d >> 1), j & 7

    row_at = []
    col_at = []
    for k in range(T):
        row_at.append(row_block(k))
        core_k, x_k, pos_k, sub_k = col_block(k)
        col_at.append(((core_k * 4 + x_k) * 4 + pos_k) * 8 + sub_k)
    tab = [jnp.full((1, 128), T, jnp.int32) for _ in range(3)]
    for k in range(T):
        row_live = jnp.where(k < live, row_at[k], -1)
        col_live = jnp.where(k < live, col_at[k], -1)
        tab[0] = jnp.where(lanes == row_live, k, tab[0])
        tab[1] = jnp.where(lanes == col_live, k, tab[1])
        tab[2] = jnp.where(lanes + 128 == col_live, k, tab[2])
        before_d = jnp.int32(T)
        before_m = jnp.int32(T)
        for q in range(k):
            before_d = jnp.where(row_at[q] == row_at[k], q, before_d)
            before_m = jnp.where(col_at[q] == col_at[k], q, before_m)
        prev_s[0, k] = before_d
        prev_s[1, k] = before_m
    table_v[...] = jnp.zeros_like(table_v)
    for q in range(3):
        table_v[q : q + 1, :] = tab[q]
    local["table"] = pltpu.make_async_copy(table_v, table_s, local_sem.at[1])
    local["table"].start()
    pd[T] = jnp.zeros((NV, B), jnp.float32)
    pm[T] = jnp.zeros((NV, B), jnp.float32)

    got("zl")
    send_y(1)

    stages = ((cx_peer, x * 2 + co), (z_peer, zh * 2 + zl), (y_peer, y))

    def share(name, buf, stage, value):
        peer, me = stages[stage]
        buf[stage, me] = value
        for d in (4, 3, 5, 2, 6, 1, 7):
            go((name, stage, d), buf.at[stage, me], buf.at[stage, me], peer(d))

    def shared(name, buf, stage):
        for d in (4, 3, 5, 2, 6, 1, 7):
            got(name, stage, d)
        total = buf[stage, 0]
        for q in range(1, 8):
            total = total + buf[stage, q]
        return total

    arrived_z()
    arrived_x(0)
    arrived_y2(0)
    for name in ("dirn", "dimg"):
        local.pop(name).wait()
    residual = cat(rbuf.at[c])
    span = jnp.concatenate([own_cd[0:8, :], residual, own_cd[8:16, :]], 0)
    known = jnp.concatenate([cimg[...], jnp.zeros_like(residual), dimg[...], span], 0)
    first = jnp.concatenate([dot(span, known, NT), jnp.zeros((24, 80), jnp.float32)], 1)

    share("early", early, 0, first)
    got("zf", 1)
    send_x(2)
    got("zf", 3)
    send_x(3)
    arrived_y2(1)
    for d in (2, 1, 3):
        go(("spz", d), own_cd, spz.at[d - 1], at(dz=d))
    go(("spl",), own_cd, spl, at(dzl=1))
    arrived_x(1)
    for way in (1, -1):
        for p in (0, 1):
            got("y1", way, p)
            got("y3", way, p)
        got("y4", way)
    share("early", early, 2, shared("early", early, 0))
    arrived_x(2)
    arrived_x(3)
    local.pop("tiles").wait()
    local.pop("table").wait()
    for g in range(4):
        for e in range(XN):
            got("core", g, e)

    for k in range(T):
        pd[k] = split_dot(cbuf[col_block(k)], tiles[list_s[2, 0, 0, k]], NT) + pd[prev_s[0, k]]

    def fill_m(half, xs):
        def step(q, carry):
            b = ((half * 4 + xs) * 4) * 8 + q
            mbuf[half, xs, q // 8, q % 8] = pm[table_s[1 + b // 128, b % 128]]
            return carry

        lax.fori_loop(0, 32, step, 0, unroll=8)

    def fill_d(q, carry):
        dbuf[q // 8, q % 8] = pd[table_s[0, q]]
        return carry

    def add(ref, *others):
        total = ref[...]
        for other in others:
            total = total + other[...]
        ref[...] = total

    def dpair(dy):
        return dbuf.at[pl.ds(((y + dy) % 8) * 2, 2)]

    lax.fori_loop(0, 128, fill_d, 0, unroll=8)
    for way in (1, -1):
        w = (1 - way) // 2
        go(("r3", way), dpair(3 * way), ry3.at[w], at(dy=way))
        go(("r4", way), dbuf.at[((y + 4) % 8) * 2 + (zl + w) % 2], ry4.at[w], at(dy=2 * way))
    for k in range(T):
        i = row_block(k)
        pm[k] = split_dot(rbuf[i >> 3, i & 7], tiles[list_s[2, 0, 0, k]], NN) + pm[prev_s[1, k]]
    for e in (2, 1, 3, 0):
        xs = (x + e) % 4
        fill_m(1 - co, xs)
        go(("rcore", e), mbuf.at[1 - co, xs], rcore.at[xs], at(dco=1))
    for way in (1, -1):
        go(("r1", way), dpair(way), ry1.at[(1 - way) // 2], at(dy=way))
    for e in (2, 1, 3, 0):
        xs = (x + e) % 4
        fill_m(co, xs)
        got("rcore", e)
        add(mbuf.at[co, xs], rcore.at[xs])
        if e == 2:
            for d in (1, 3):
                go(("zx", d), mbuf.at[co, xs, pos[d]], zx.at[d // 2], at(dz=-d))
            go(("rx2", 3), mbuf.at[co, xs, 3], rx2.at[1], at(dx=2))
        elif e:
            go(("rx", e), mbuf.at[co, xs], rx.at[e // 2], at(dx=e))
    got("spl")
    share("early", early, 1, shared("early", early, 2))
    far = mbuf.at[co, (x + 2) % 4, 0]
    for d in (1, 3):
        got("zx", d)
    add(far, zx.at[0], zx.at[1])
    go(("rx2", 0), far, rx2.at[0], at(dx=2))

    for way in (1, -1):
        w = (1 - way) // 2
        got("r3", way)
        got("r4", way)
        add(dpair(2 * way), ry3.at[w])
        add(dbuf.at[((y + 2 * way) % 8) * 2 + (zl + w) % 2], ry4.at[w])
        go(("r2", way), dpair(2 * way), ry2.at[w], at(dy=2 * way))

    total = shared("early", early, 1)
    at_row = lax.broadcasted_iota(jnp.int32, (24, 24), 0)
    at_col = lax.broadcasted_iota(jnp.int32, (24, 24), 1)
    eye = jnp.where(at_row == at_col, 1.0, 0.0).astype(jnp.float32)
    left, inverse = total[:, 24:48], eye
    for k in range(24):
        root = jnp.sqrt(left[k : k + 1, k : k + 1])
        row = left[k : k + 1, :] / root
        row_inverse = inverse[k : k + 1, :] / root
        factor = left[:, k : k + 1] / root
        left = jnp.where(at_row > k, left - factor * row, jnp.where(at_row == k, row, left))
        inverse = jnp.where(
            at_row > k, inverse - factor * row_inverse, jnp.where(at_row == k, row_inverse, inverse)
        )
    white_known = dot(dot(inverse, total[:, 0:24], NN), inverse, NT)

    for d in (1, 2, 3):
        got("spz", d)
    for e in (1, 3):
        got("rx", e)
    for q in (0, 3):
        got("rx2", q)
    add(mbuf.at[co, x], rx.at[0], rx.at[1])
    add(mbuf.at[co, x, 0], rx2.at[0])
    add(mbuf.at[co, x, 3], rx2.at[1])
    for d in (2, 1, 3):
        go(("rz", d), mbuf.at[co, x, pos[d]], rz.at[d - 1], at(dz=-d))
    for step in ("r1", "r2"):
        for way in (1, -1):
            got(step, way)
    add(dpair(0), ry1.at[0], ry1.at[1], ry2.at[0], ry2.at[1])
    other_c = y * 2 + (1 - zl)
    go(("rzl",), dbuf.at[other_c], rzl, at(dzl=1))

    local.pop("en").wait()
    for s in range(SUB):
        cols = slice(s * B, (s + 1) * B)
        applied[:, cols] = en[:, cols] * rbuf[c, s] + (dbuf[c, s] + mbuf[co, x, 0, s])

    def partial_gram(image, own_span, res):
        return dot(image, jnp.concatenate([own_span[0:8, :], res, own_span[8:16, :]], 0), NT)

    gram = partial_gram(applied[...], own_cd, cat(rbuf.at[c]))
    gram = gram + partial_gram(cat(dbuf.at[other_c]), spl, cat(rbuf.at[other_c]))
    for d in (1, 2, 3):
        gram = gram + partial_gram(cat(mbuf.at[co, x, pos[d]]), spz.at[d - 1], cat(cbuf.at[co, x, pos[d]]))
    gram = jnp.concatenate([gram, jnp.zeros((NV, 104), jnp.float32)], 1)

    share("late", late, 0, gram)
    share("late", late, 2, shared("late", late, 0))
    gram = shared("late", late, 2)
    share("late", late, 1, gram)

    for d in (1, 3, 2):
        got("rz", d)
    got("rzl")
    for s in range(SUB):
        cols = slice(s * B, (s + 1) * B)
        applied[:, cols] = applied[:, cols] + (rzl[s] + (rz[0, s] + rz[1, s] + rz[2, s]))
    gram = shared("late", late, 1)[:, 0:24]

    white_all = white_known + dot(inverse[:, 8:16], dot(gram, inverse, NT), NN)
    whitened = 0.5 * (white_all + dot(white_all, eye, TN))
    white[...] = 0.5 * (whitened + dot(whitened, eye, TN))

    for copy in copies.values():
        copy.wait_send()


def finish(applied, white, applied_out, white_out, sems):
    first = pltpu.make_async_copy(applied, applied_out, sems.at[0])
    second = pltpu.make_async_copy(white, white_out, sems.at[1])
    first.start()
    second.start()
    first.wait()
    second.wait()


def body(
    tile_data, tile_list, tile_count, current, current_image, direction, direction_image,
    energies, precond, ritz_prev,
):
    vmem = pl.BlockSpec(memory_space=pltpu.VMEM)
    hbm = pl.BlockSpec(memory_space=pltpu.HBM)
    f32 = jnp.float32
    n_ids = len(IDS)
    applied, white = pl.pallas_call(
        kernel,
        out_shape=(pltpu.VMEM(current.shape, f32), pltpu.VMEM((24, 24), f32)),
        in_specs=[hbm] * 10,
        out_specs=(vmem, vmem),
        scratch_shapes=[
            pltpu.SMEM(tile_list.shape, jnp.int32),
            pltpu.SMEM((1, 1), jnp.int32),
            pltpu.VMEM((2 * NV, SUB * B), f32),
            pltpu.VMEM(current.shape, f32),
            pltpu.VMEM(current.shape, f32),
            pltpu.VMEM((1, SUB * B), f32),
            pltpu.VMEM((1, SUB * B), f32),
            pltpu.SMEM((NV,), f32),
            pltpu.VMEM((T, B, B), jnp.bfloat16),
            pltpu.VMEM((16, SUB, NV, B), f32),
            pltpu.VMEM((2, XN, ZH, SUB, NV, B), f32),
            pltpu.VMEM((16, SUB, NV, B), f32),
            pltpu.VMEM((2, XN, ZH, SUB, NV, B), f32),
            pltpu.VMEM((2, 2, SUB, NV, B), f32),
            pltpu.VMEM((2, 2, SUB, NV, B), f32),
            pltpu.VMEM((2, 2, SUB, NV, B), f32),
            pltpu.VMEM((2, SUB, NV, B), f32),
            pltpu.VMEM((XN, ZH, SUB, NV, B), f32),
            pltpu.VMEM((2, ZH, SUB, NV, B), f32),
            pltpu.VMEM((2, SUB, NV, B), f32),
            pltpu.VMEM((2, SUB, NV, B), f32),
            pltpu.VMEM((3, SUB, NV, B), f32),
            pltpu.VMEM((SUB, NV, B), f32),
            pltpu.VMEM((3, 2 * NV, SUB * B), f32),
            pltpu.VMEM((2 * NV, SUB * B), f32),
            pltpu.VMEM((T + 1, NV, B), f32),
            pltpu.VMEM((T + 1, NV, B), f32),
            pltpu.VMEM((3, 8, 24, 128), f32),
            pltpu.VMEM((3, 8, NV, 128), f32),
            pltpu.VMEM((8, 128), jnp.int32),
            pltpu.SMEM((8, 128), jnp.int32),
            pltpu.SMEM((2, T), jnp.int32),
            pltpu.SemaphoreType.DMA((n_ids,)),
            pltpu.SemaphoreType.DMA((n_ids,)),
            pltpu.SemaphoreType.DMA((12,)),
        ],
        compiler_params=pltpu.CompilerParams(
            collective_id=0, has_side_effects=True, vmem_limit_bytes=60 * 1024 * 1024
        ),
        name="lobpcg_step",
    )(
        tile_data, tile_list, tile_count, current, current_image, direction, direction_image,
        energies.reshape(1, -1), precond.reshape(1, -1), ritz_prev,
    )
    return (applied, white)


def solution(mesh):
    in_specs = (
        P("row", "col", None, None, None),
        P(None, "row", "col", None),
        P("row", "col"),
        P(None, ("row", "col")),
        P(None, ("row", "col")),
        P(None, ("row", "col")),
        P(None, ("row", "col")),
        P(("row", "col")),
        P(("row", "col")),
        P(),
    )
    out_specs = (P(None, ("row", "col")), P())
    return jax.shard_map(body, mesh=mesh, in_specs=in_specs, out_specs=out_specs, check_vma=False)
```

```python
import jax
import jax.numpy as jnp
from jax import lax
from jax.experimental import pallas as pl
from jax.experimental.pallas import tpu as pltpu
from jax.sharding import PartitionSpec as P

MESH = pl.DeviceIdType.MESH
HIGHEST = lax.Precision.HIGHEST
ZH, XN, YN = 4, 4, 8
NV, B, SUB, T = 8, 256, 8, 12
NT = (((1,), (1,)), ((), ()))
NN = (((1,), (0,)), ((), ()))
TN = (((0,), (0,)), ((), ()))

IDS = {}


def idx(*name):
    return IDS.setdefault(name, len(IDS))


def fill_ids():
    idx("zl")
    idx("rzl")
    idx("spl")
    for way in (1, -1):
        for p in (0, 1):
            for step in ("y1", "y2", "y3", "r1", "r2", "r3"):
                idx(step, way, p)
        for step in ("y4", "r4"):
            idx(step, way)
    for d in (1, 3):
        idx("zf", d)
        idx("zx", d)
    idx("rx2", 0)
    idx("rx2", 3)
    for d in range(1, ZH):
        idx("z", d)
        idx("rz", d)
        idx("spz", d)
    for e in range(XN):
        idx("rx", e)
        for g in range(4):
            idx("x", g, e)
    idx("codes")
    idx("need")
    idx("raw")
    for stage in range(3):
        for d in range(1, 8):
            idx("early", stage, d)
            idx("late", stage, d)


fill_ids()


def split3(v):
    hi = v.astype(jnp.bfloat16).astype(jnp.float32)
    rest = v - hi
    mid = rest.astype(jnp.bfloat16).astype(jnp.float32)
    low = rest - mid
    return jnp.concatenate([hi, mid, low], 0).astype(jnp.bfloat16)


def split_dot(v, tile, dims):
    out = lax.dot_general(split3(v), tile, dims, preferred_element_type=jnp.float32)
    return (out[16:24] + out[8:16]) + out[0:8]


def dot(a, b, dims):
    return lax.dot_general(a, b, dims, precision=HIGHEST, preferred_element_type=jnp.float32)


def cat(ref):
    return jnp.concatenate([ref[s] for s in range(SUB)], 1)


def kernel(
    tile_hbm, list_hbm, count_hbm, cur_hbm, cimg_hbm, dirn_hbm, dimg_hbm, en_hbm, pre_hbm, ritz_hbm,
    applied, white,
    list_s, count_s, own_cd, cimg, dimg, en, pre, ritz_s, tiles, rbuf, cbuf, dbuf, mbuf,
    ry1, ry2, ry3, ry4, rx, rx2, zx, rz, rzl, spz, spl, pd, raw, pm, pack, given, early, late,
    table_v, table_s, prev_s, code_v, other_v, other_s, send, recv, local_sem,
):
    r = lax.axis_index("row")
    c = lax.axis_index("col")
    zh, x, co = r // 8, (r // 2) % 4, r % 2
    y, zl = c // 2, c % 2

    def dev(zh_, x_, co_, y_, zl_):
        return ((zh_ * 4 + x_) * 2 + co_, y_ * 2 + zl_)

    def at(dz=0, dx=0, dco=0, dy=0, dzl=0):
        return dev((zh + dz) % 4, (x + dx) % 4, (co + dco) % 2, (y + dy) % 8, (zl + dzl) % 2)

    def cx_peer(d):
        q = (x * 2 + co + d) % 8
        return dev(zh, q // 2, q % 2, y, zl)

    def z_peer(d):
        q = (zh * 2 + zl + d) % 8
        return dev(q // 2, x, co, y, q % 2)

    def y_peer(d):
        return dev(zh, x, co, (y + d) % 8, zl)

    local = {}

    def load(*items):
        for name, src, dst in items:
            local[name] = pltpu.make_async_copy(src, dst, local_sem.at[2 + len(local)])
            local[name].start()

    load(
        ("cimg", cimg_hbm, cimg), ("cur", cur_hbm, own_cd.at[0:8]), ("pre", pre_hbm, pre), ("ritz", ritz_hbm, ritz_s),
    )
    barrier = pltpu.get_barrier_semaphore()
    near = [at(dz=1), at(dz=3), at(dy=2), at(dy=6), at(dx=2), at(dzl=1), at(dy=1), at(dy=7), at(dx=1), at(dx=3), at(dco=1)]
    for peer in near:
        pl.semaphore_signal(barrier, inc=1, device_id=peer, device_id_type=MESH)

    load(
        ("list", list_hbm, list_s), ("count", count_hbm, count_s), ("dirn", dirn_hbm, own_cd.at[8:16]),
        ("dimg", dimg_hbm, dimg), ("en", en_hbm, en), ("tiles", tile_hbm.at[0, 0], tiles),
    )
    copies = {}

    def go(name, src, dst, target):
        k = idx(*name)
        copy = pltpu.make_async_remote_copy(
            src_ref=src, dst_ref=dst, send_sem=send.at[k], recv_sem=recv.at[k],
            device_id=target, device_id_type=MESH,
        )
        copy.start()
        copies[name] = copy

    def got(*name):
        copies[name].wait_recv()

    for name in ("ritz", "cimg", "cur", "pre"):
        local.pop(name).wait()
    rows = lax.broadcasted_iota(jnp.int32, (NV, B), 0)
    ritz = jnp.zeros((NV, B), jnp.float32)
    for a in range(NV):
        ritz = jnp.where(rows == a, ritz_s[a], ritz)
    for s in range(SUB):
        cols = slice(s * B, (s + 1) * B)
        piece = pre[:, cols] * (cimg[:, cols] - ritz * own_cd[0:8, cols])
        rbuf[c, s] = piece
        cbuf[x * 32 + s] = piece

    pl.semaphore_wait(barrier, len(near))

    pos = (0, 1, 3, 2)
    group = ((0, 8), (8, 16), (24, 4), (28, 4))

    def rpiece(dy, p):
        return rbuf.at[((y + dy) % 8) * 2 + (zl + p) % 2]

    def send_y(p):
        for step, hops in (("y2", 2), ("y1", 1)):
            for way in (1, -1):
                go((step, way, p), rpiece(0, p), rpiece(0, p), at(dy=hops * way))

    def arrived_y2(p):
        for way in (1, -1):
            got("y2", way, p)
            piece = rpiece(-2 * way, p)
            if p == (1 - way) // 2:
                go(("y4", way), piece, piece, at(dy=2 * way))
            go(("y3", way, p), piece, piece, at(dy=way))

    def cpart(dx, first, size):
        return cbuf.at[pl.ds(((x + dx) % 4) * 32 + first, size)]

    def send_x(g):
        part = cpart(0, *group[g])
        for e in (2, 1, 3):
            go(("x", g, e), part, part, at(dx=e))

    def arrived_x(g):
        for e in (1, 3, 2):
            got("x", g, e)

    own = rpiece(0, 0)
    own_c = cpart(0, 0, 8)
    go(("zl",), own, own, at(dzl=1))
    for d in (1, 3):
        go(("z", d), own_c, cpart(0, 8 * pos[d], 8), at(dz=d))
    send_y(0)
    send_x(0)

    def arrived_z():
        for d in (1, 3):
            got("z", d)
            half = 0 if d == 1 else 4
            go(("zf", d), cpart(0, 8 * pos[d] + half, 4), cpart(0, 24 + half, 4), at(dz=d))
        send_x(1)

    local.pop("list").wait()
    local.pop("count").wait()
    lanes = lax.broadcasted_iota(jnp.int32, (1, 128), 1)
    live = count_s[0, 0]

    def row_block(k):
        return list_s[0, 0, 0, k] & 127

    def col_code(k):
        j = list_s[1, 0, 0, k]
        owner = j >> 7
        d = (zh - (owner >> 3)) & 3
        return (owner & 1) * 128 + (((owner >> 1) & 3) * 4 + (d ^ (d >> 1))) * 8 + (j & 7)

    codes = [col_code(k) for k in range(T)]
    code_row = jnp.zeros((8, 128), jnp.int32)
    lanes8 = lax.broadcasted_iota(jnp.int32, (8, 128), 1)
    for k in range(T):
        code_row = jnp.where(lanes8 == k, codes[k], code_row)
    code_v[...] = code_row
    go(("codes",), code_v, other_v, at(dco=1))

    def last_of(keys):
        found = []
        for k in range(len(keys)):
            before = jnp.int32(len(keys))
            for q in range(k):
                before = jnp.where(keys[q] == keys[k], q, before)
            found.append(before)
        return found

    def table_of(keys):
        out = jnp.full((1, 128), len(keys), jnp.int32)
        for k, key in enumerate(keys):
            out = jnp.where(lanes == key, k, out)
        return out

    row_at = [row_block(k) for k in range(T)]
    for k, before in enumerate(last_of(row_at)):
        prev_s[0, k] = before
    table_v[...] = jnp.zeros_like(table_v)
    table_v[0:1, :] = table_of(row_at)
    pd[T] = jnp.zeros((NV, B), jnp.float32)
    pm[2 * T] = jnp.zeros((NV, B), jnp.float32)

    got("zl")
    send_y(1)

    stages = ((cx_peer, x * 2 + co), (z_peer, zh * 2 + zl), (y_peer, y))

    def share(name, buf, stage, value):
        peer, me = stages[stage]
        buf[stage, me] = value
        for d in (4, 3, 5, 2, 6, 1, 7):
            go((name, stage, d), buf.at[stage, me], buf.at[stage, me], peer(d))

    def shared(name, buf, stage):
        for d in (4, 3, 5, 2, 6, 1, 7):
            got(name, stage, d)
        total = buf[stage, 0]
        for q in range(1, 8):
            total = total + buf[stage, q]
        return total

    arrived_z()
    got("codes")
    local["codes"] = pltpu.make_async_copy(other_v, other_s, local_sem.at[0])
    local["codes"].start()
    arrived_x(0)
    arrived_y2(0)
    for name in ("dirn", "dimg"):
        local.pop(name).wait()
    residual = cat(rbuf.at[c])
    span = jnp.concatenate([own_cd[0:8, :], residual, own_cd[8:16, :]], 0)
    known = jnp.concatenate([cimg[...], jnp.zeros_like(residual), dimg[...], span], 0)
    first = jnp.concatenate([dot(span, known, NT), jnp.zeros((24, 80), jnp.float32)], 1)

    share("early", early, 0, first)
    got("zf", 1)
    send_x(2)
    got("zf", 3)
    send_x(3)
    arrived_y2(1)
    go(("spz", 2), own_cd, spz.at[1], at(dz=2))
    go(("spl",), own_cd, spl, at(dzl=1))
    arrived_x(1)
    local.pop("codes").wait()
    other_codes = [other_s[0, k] for k in range(T)]
    keys = [jnp.where(code >> 7 == co, code & 127, -1 - k) for k, code in enumerate(codes + other_codes)]
    for k, before in enumerate(last_of(keys)):
        prev_s[1, k] = before
    table_v[1:2, :] = table_of(keys)
    local["table"] = pltpu.make_async_copy(table_v, table_s, local_sem.at[1])
    local["table"].start()
    share("early", early, 2, shared("early", early, 0))
    arrived_x(2)
    arrived_x(3)
    for k in range(T):
        pack[k] = cbuf[other_codes[k] & 127]
    go(("need",), pack, given, at(dco=1))
    for d in (1, 3):
        go(("spz", d), own_cd, spz.at[d - 1], at(dz=d))
    local.pop("tiles").wait()
    local.pop("table").wait()
    got("need")

    for k in range(T):
        source = jnp.where(codes[k] >> 7 == co, cbuf[codes[k] & 127], given[k])
        product = split_dot(source, tiles[list_s[2, 0, 0, k]], NT)
        pd[k] = jnp.where(k < live, product, 0.0) + pd[prev_s[0, k]]

    def fill_m(xs):
        def step(q, carry):
            mbuf[xs * 32 + q] = pm[table_s[1, xs * 32 + q]]
            return carry

        lax.fori_loop(0, 32, step, 0, unroll=8)

    def fill_d(q, carry):
        dbuf[q // 8, q % 8] = pd[table_s[0, q]]
        return carry

    def add(ref, *others):
        total = ref[...]
        for other in others:
            total = total + other[...]
        ref[...] = total

    lax.fori_loop(0, 128, fill_d, 0, unroll=8)

    def dpiece(dy, p):
        return dbuf.at[((y + dy) % 8) * 2 + (zl + p) % 2]

    def send_r(step, hops, at_y, way, p, buf):
        go((step, way, p), dpiece(at_y * way, p), buf.at[(1 - way) // 2, p], at(dy=hops * way))

    for way in (1, -1):
        send_r("r3", 1, 3, way, (1 + way) // 2, ry3)
    for way in (1, -1):
        w = (1 - way) // 2
        go(("r4", way), dpiece(4, w), ry4.at[w], at(dy=2 * way))
        send_r("r3", 1, 3, way, w, ry3)

    for way in (1, -1):
        for p in (0, 1):
            got("y1", way, p)
            got("y3", way, p)
        got("y4", way)
    for k in range(T):
        i = row_block(k)
        product = split_dot(rbuf[i >> 3, i & 7], tiles[list_s[2, 0, 0, k]], NN)
        raw[k] = jnp.where(k < live, product, 0.0)
    go(("raw",), raw.at[pl.ds(0, T)], raw.at[pl.ds(T, T)], at(dco=1))
    for way in (1, -1):
        p = (1 + way) // 2
        got("r3", way, p)
        add(dpiece(2 * way, p), ry3.at[(1 - way) // 2, p])
        send_r("r2", 2, 2, way, p, ry2)

    def mpart(dx, first, size):
        return mbuf.at[pl.ds(((x + dx) % 4) * 32 + first, size)]

    got("raw")
    for k in range(2 * T):
        pm[k] = raw[k] + pm[prev_s[1, k]]
    for e in (2, 1, 3, 0):
        fill_m((x + e) % 4)
        if e == 2:
            for d in (1, 3):
                go(("zx", d), mpart(2, 8 * pos[d], 8), zx.at[d // 2], at(dz=-d))
            go(("rx2", 3), mpart(2, 24, 8), rx2.at[1], at(dx=2))
        elif e:
            go(("rx", e), mpart(e, 0, 32), rx.at[e // 2], at(dx=e))
    for way in (1, -1):
        w = (1 - way) // 2
        for p in (0, 1):
            send_r("r1", 1, 1, way, p, ry1)
    got("spl")
    share("early", early, 1, shared("early", early, 2))
    far = mpart(2, 0, 8)
    for d in (1, 3):
        got("zx", d)
    add(far, zx.at[0], zx.at[1])
    go(("rx2", 0), far, rx2.at[0], at(dx=2))

    for way in (1, -1):
        w = (1 - way) // 2
        got("r3", way, w)
        got("r4", way)
        add(dpiece(2 * way, w), ry3.at[w, w], ry4.at[w])
        send_r("r2", 2, 2, way, w, ry2)

    total = shared("early", early, 1)
    at_row = lax.broadcasted_iota(jnp.int32, (24, 24), 0)
    at_col = lax.broadcasted_iota(jnp.int32, (24, 24), 1)
    eye = jnp.where(at_row == at_col, 1.0, 0.0).astype(jnp.float32)
    left, inverse = total[:, 24:48], eye
    for k in range(24):
        root = jnp.sqrt(left[k : k + 1, k : k + 1])
        row = left[k : k + 1, :] / root
        row_inverse = inverse[k : k + 1, :] / root
        factor = left[:, k : k + 1] / root
        left = jnp.where(at_row > k, left - factor * row, jnp.where(at_row == k, row, left))
        inverse = jnp.where(
            at_row > k, inverse - factor * row_inverse, jnp.where(at_row == k, row_inverse, inverse)
        )
    white_known = dot(dot(inverse, total[:, 0:24], NN), inverse, NT)

    for d in (1, 2, 3):
        got("spz", d)
    for e in (1, 3):
        got("rx", e)
    for q in (0, 3):
        got("rx2", q)
    add(mpart(0, 0, 32), rx.at[0], rx.at[1])
    add(mpart(0, 0, 8), rx2.at[0])
    add(mpart(0, 24, 8), rx2.at[1])
    for d in (2, 1, 3):
        go(("rz", d), mpart(0, 8 * pos[d], 8), rz.at[d - 1], at(dz=-d))
    for way in (1, -1):
        for p in (0, 1):
            got("r1", way, p)
            got("r2", way, p)
    for p in (0, 1):
        add(dpiece(0, p), ry1.at[0, p], ry1.at[1, p], ry2.at[0, p], ry2.at[1, p])
    other_c = y * 2 + (1 - zl)
    go(("rzl",), dbuf.at[other_c], rzl, at(dzl=1))

    local.pop("en").wait()
    for s in range(SUB):
        cols = slice(s * B, (s + 1) * B)
        applied[:, cols] = en[:, cols] * rbuf[c, s] + (dbuf[c, s] + mbuf[x * 32 + s])

    def partial_gram(image, own_span, res):
        return dot(image, jnp.concatenate([own_span[0:8, :], res, own_span[8:16, :]], 0), NT)

    gram = partial_gram(applied[...], own_cd, cat(rbuf.at[c]))
    gram = gram + partial_gram(cat(dbuf.at[other_c]), spl, cat(rbuf.at[other_c]))
    for d in (1, 2, 3):
        gram = gram + partial_gram(cat(mpart(0, 8 * pos[d], 8)), spz.at[d - 1], cat(cpart(0, 8 * pos[d], 8)))
    gram = jnp.concatenate([gram, jnp.zeros((NV, 104), jnp.float32)], 1)

    share("late", late, 0, gram)
    share("late", late, 2, shared("late", late, 0))
    gram = shared("late", late, 2)
    share("late", late, 1, gram)

    for d in (1, 3, 2):
        got("rz", d)
    got("rzl")
    for s in range(SUB):
        cols = slice(s * B, (s + 1) * B)
        applied[:, cols] = applied[:, cols] + (rzl[s] + (rz[0, s] + rz[1, s] + rz[2, s]))
    gram = shared("late", late, 1)[:, 0:24]

    white_all = white_known + dot(inverse[:, 8:16], dot(gram, inverse, NT), NN)
    whitened = 0.5 * (white_all + dot(white_all, eye, TN))
    white[...] = 0.5 * (whitened + dot(whitened, eye, TN))

    for copy in copies.values():
        copy.wait_send()


def finish(applied, white, applied_out, white_out, sems):
    first = pltpu.make_async_copy(applied, applied_out, sems.at[0])
    second = pltpu.make_async_copy(white, white_out, sems.at[1])
    first.start()
    second.start()
    first.wait()
    second.wait()


def body(
    tile_data, tile_list, tile_count, current, current_image, direction, direction_image,
    energies, precond, ritz_prev,
):
    vmem = pl.BlockSpec(memory_space=pltpu.VMEM)
    hbm = pl.BlockSpec(memory_space=pltpu.HBM)
    f32 = jnp.float32
    n_ids = len(IDS)
    applied, white = pl.pallas_call(
        kernel,
        out_shape=(pltpu.VMEM(current.shape, f32), pltpu.VMEM((24, 24), f32)),
        in_specs=[hbm] * 10,
        out_specs=(vmem, vmem),
        scratch_shapes=[
            pltpu.SMEM(tile_list.shape, jnp.int32),
            pltpu.SMEM((1, 1), jnp.int32),
            pltpu.VMEM((2 * NV, SUB * B), f32),
            pltpu.VMEM(current.shape, f32),
            pltpu.VMEM(current.shape, f32),
            pltpu.VMEM((1, SUB * B), f32),
            pltpu.VMEM((1, SUB * B), f32),
            pltpu.SMEM((NV,), f32),
            pltpu.VMEM((T, B, B), jnp.bfloat16),
            pltpu.VMEM((16, SUB, NV, B), f32),
            pltpu.VMEM((XN * ZH * SUB, NV, B), f32),
            pltpu.VMEM((16, SUB, NV, B), f32),
            pltpu.VMEM((XN * ZH * SUB, NV, B), f32),
            pltpu.VMEM((2, 2, SUB, NV, B), f32),
            pltpu.VMEM((2, 2, SUB, NV, B), f32),
            pltpu.VMEM((2, 2, SUB, NV, B), f32),
            pltpu.VMEM((2, SUB, NV, B), f32),
            pltpu.VMEM((2, ZH * SUB, NV, B), f32),
            pltpu.VMEM((2, SUB, NV, B), f32),
            pltpu.VMEM((2, SUB, NV, B), f32),
            pltpu.VMEM((3, SUB, NV, B), f32),
            pltpu.VMEM((SUB, NV, B), f32),
            pltpu.VMEM((3, 2 * NV, SUB * B), f32),
            pltpu.VMEM((2 * NV, SUB * B), f32),
            pltpu.VMEM((T + 1, NV, B), f32),
            pltpu.VMEM((2 * T, NV, B), f32),
            pltpu.VMEM((2 * T + 1, NV, B), f32),
            pltpu.VMEM((T, NV, B), f32),
            pltpu.VMEM((T, NV, B), f32),
            pltpu.VMEM((3, 8, 24, 128), f32),
            pltpu.VMEM((3, 8, NV, 128), f32),
            pltpu.VMEM((8, 128), jnp.int32),
            pltpu.SMEM((8, 128), jnp.int32),
            pltpu.SMEM((2, 2 * T), jnp.int32),
            pltpu.VMEM((8, 128), jnp.int32),
            pltpu.VMEM((8, 128), jnp.int32),
            pltpu.SMEM((8, 128), jnp.int32),
            pltpu.SemaphoreType.DMA((n_ids,)),
            pltpu.SemaphoreType.DMA((n_ids,)),
            pltpu.SemaphoreType.DMA((12,)),
        ],
        compiler_params=pltpu.CompilerParams(
            collective_id=0, has_side_effects=True, vmem_limit_bytes=60 * 1024 * 1024
        ),
        name="lobpcg_step",
    )(
        tile_data, tile_list, tile_count, current, current_image, direction, direction_image,
        energies.reshape(1, -1), precond.reshape(1, -1), ritz_prev,
    )
    return (applied, white)


def solution(mesh):
    in_specs = (
        P("row", "col", None, None, None),
        P(None, "row", "col", None),
        P("row", "col"),
        P(None, ("row", "col")),
        P(None, ("row", "col")),
        P(None, ("row", "col")),
        P(None, ("row", "col")),
        P(("row", "col")),
        P(("row", "col")),
        P(),
    )
    out_specs = (P(None, ("row", "col")), P())
    return jax.shard_map(body, mesh=mesh, in_specs=in_specs, out_specs=out_specs, check_vma=False)
```

```python
import jax
import jax.numpy as jnp
from jax import lax
from jax.experimental import pallas as pl
from jax.experimental.pallas import tpu as pltpu
from jax.sharding import PartitionSpec as P

MESH = pl.DeviceIdType.MESH
HIGHEST = lax.Precision.HIGHEST
ZH, XN, YN = 4, 4, 8
NV, B, SUB, T = 8, 256, 8, 12
NT = (((1,), (1,)), ((), ()))
NN = (((1,), (0,)), ((), ()))
TN = (((0,), (0,)), ((), ()))

IDS = {}


def idx(*name):
    return IDS.setdefault(name, len(IDS))


def fill_ids():
    idx("zl")
    idx("rzl")
    idx("spl")
    for way in (1, -1):
        for p in (0, 1):
            for step in ("y1", "y2", "y3", "r1", "r2", "r3"):
                idx(step, way, p)
        for step in ("y4", "r4"):
            idx(step, way)
    for d in (1, 3):
        idx("zf", d)
        idx("zx", d)
    idx("rx2", 0)
    idx("rx2", 3)
    for d in range(1, ZH):
        idx("z", d)
        idx("rz", d)
        idx("spz", d)
    for e in range(XN):
        idx("rx", e)
        for g in range(4):
            idx("x", g, e)
    idx("codes")
    idx("need")
    idx("raw")
    for stage in range(3):
        for d in range(1, 8):
            idx("early", stage, d)
            idx("late", stage, d)


fill_ids()


def split3(v):
    hi = v.astype(jnp.bfloat16).astype(jnp.float32)
    rest = v - hi
    mid = rest.astype(jnp.bfloat16).astype(jnp.float32)
    low = rest - mid
    return jnp.concatenate([hi, mid, low], 0).astype(jnp.bfloat16)


def split_dot(v, tile, dims):
    out = lax.dot_general(split3(v), tile, dims, preferred_element_type=jnp.float32)
    return (out[16:24] + out[8:16]) + out[0:8]


def dot(a, b, dims):
    return lax.dot_general(a, b, dims, precision=HIGHEST, preferred_element_type=jnp.float32)


def cat(ref):
    return jnp.concatenate([ref[s] for s in range(SUB)], 1)


def kernel(
    tile_hbm, list_hbm, count_hbm, cur_hbm, cimg_hbm, dirn_hbm, dimg_hbm, en_hbm, pre_hbm, ritz_hbm,
    applied, white,
    list_s, count_s, own_cd, cimg, dimg, en, pre, ritz_s, tiles, rbuf, cbuf, dbuf, mbuf,
    ry1, ry2, ry3, ry4, rx, rx2, zx, rz, rzl, spz, spl, pd, raw, pm, pack, given, early, late,
    table_v, table_s, prev_s, code_v, other_v, other_s, send, recv, local_sem,
):
    r = lax.axis_index("row")
    c = lax.axis_index("col")
    zh, x, co = r // 8, (r // 2) % 4, r % 2
    y, zl = c // 2, c % 2

    def dev(zh_, x_, co_, y_, zl_):
        return ((zh_ * 4 + x_) * 2 + co_, y_ * 2 + zl_)

    def at(dz=0, dx=0, dco=0, dy=0, dzl=0):
        return dev((zh + dz) % 4, (x + dx) % 4, (co + dco) % 2, (y + dy) % 8, (zl + dzl) % 2)

    def cx_peer(d):
        q = (x * 2 + co + d) % 8
        return dev(zh, q // 2, q % 2, y, zl)

    def z_peer(d):
        q = (zh * 2 + zl + d) % 8
        return dev(q // 2, x, co, y, q % 2)

    def y_peer(d):
        return dev(zh, x, co, (y + d) % 8, zl)

    local = {}

    def load(*items):
        for name, src, dst in items:
            local[name] = pltpu.make_async_copy(src, dst, local_sem.at[2 + len(local)])
            local[name].start()

    load(
        ("cimg", cimg_hbm, cimg), ("cur", cur_hbm, own_cd.at[0:8]), ("pre", pre_hbm, pre), ("ritz", ritz_hbm, ritz_s),
    )
    barrier = pltpu.get_barrier_semaphore()
    near = [at(dz=1), at(dz=3), at(dy=2), at(dy=6), at(dx=2), at(dzl=1), at(dy=1), at(dy=7), at(dx=1), at(dx=3), at(dco=1)]
    for peer in near:
        pl.semaphore_signal(barrier, inc=1, device_id=peer, device_id_type=MESH)

    load(
        ("list", list_hbm, list_s), ("count", count_hbm, count_s), ("dirn", dirn_hbm, own_cd.at[8:16]),
        ("dimg", dimg_hbm, dimg), ("en", en_hbm, en), ("tiles", tile_hbm.at[0, 0], tiles),
    )
    copies = {}

    def go(name, src, dst, target):
        k = idx(*name)
        copy = pltpu.make_async_remote_copy(
            src_ref=src, dst_ref=dst, send_sem=send.at[k], recv_sem=recv.at[k],
            device_id=target, device_id_type=MESH,
        )
        copy.start()
        copies[name] = copy

    def got(*name):
        copies[name].wait_recv()

    for name in ("ritz", "cimg", "cur", "pre"):
        local.pop(name).wait()
    rows = lax.broadcasted_iota(jnp.int32, (NV, B), 0)
    ritz = jnp.zeros((NV, B), jnp.float32)
    for a in range(NV):
        ritz = jnp.where(rows == a, ritz_s[a], ritz)
    for s in range(SUB):
        cols = slice(s * B, (s + 1) * B)
        piece = pre[:, cols] * (cimg[:, cols] - ritz * own_cd[0:8, cols])
        rbuf[c, s] = piece
        cbuf[x * 32 + s] = piece

    pl.semaphore_wait(barrier, len(near))

    pos = (0, 1, 3, 2)
    group = ((0, 8), (8, 16), (24, 4), (28, 4))

    def rpiece(dy, p):
        return rbuf.at[((y + dy) % 8) * 2 + (zl + p) % 2]

    def send_y(p):
        for step, hops in (("y2", 2), ("y1", 1)):
            for way in (1, -1):
                go((step, way, p), rpiece(0, p), rpiece(0, p), at(dy=hops * way))

    def arrived_y2(p):
        for way in (1, -1):
            got("y2", way, p)
            piece = rpiece(-2 * way, p)
            if p == (1 - way) // 2:
                go(("y4", way), piece, piece, at(dy=2 * way))
            go(("y3", way, p), piece, piece, at(dy=way))

    def cpart(dx, first, size):
        return cbuf.at[pl.ds(((x + dx) % 4) * 32 + first, size)]

    def send_x(g):
        part = cpart(0, *group[g])
        for e in (2, 1, 3):
            go(("x", g, e), part, part, at(dx=e))

    def arrived_x(g):
        for e in (1, 3, 2):
            got("x", g, e)

    own = rpiece(0, 0)
    own_c = cpart(0, 0, 8)
    go(("zl",), own, own, at(dzl=1))
    for d in (1, 3):
        go(("z", d), own_c, cpart(0, 8 * pos[d], 8), at(dz=d))
    send_y(0)
    send_x(0)

    def arrived_z():
        for d in (1, 3):
            got("z", d)
            half = 0 if d == 1 else 4
            go(("zf", d), cpart(0, 8 * pos[d] + half, 4), cpart(0, 24 + half, 4), at(dz=d))
        send_x(1)

    local.pop("list").wait()
    local.pop("count").wait()
    lanes = lax.broadcasted_iota(jnp.int32, (1, 128), 1)
    live = count_s[0, 0]

    def row_block(k):
        return list_s[0, 0, 0, k] & 127

    def col_code(k):
        j = list_s[1, 0, 0, k]
        owner = j >> 7
        d = (zh - (owner >> 3)) & 3
        return (owner & 1) * 128 + (((owner >> 1) & 3) * 4 + (d ^ (d >> 1))) * 8 + (j & 7)

    codes = [col_code(k) for k in range(T)]
    code_row = jnp.zeros((8, 128), jnp.int32)
    lanes8 = lax.broadcasted_iota(jnp.int32, (8, 128), 1)
    for k in range(T):
        code_row = jnp.where(lanes8 == k, codes[k], code_row)
    code_v[...] = code_row
    go(("codes",), code_v, other_v, at(dco=1))

    def last_of(keys):
        found = []
        for k in range(len(keys)):
            before = jnp.int32(len(keys))
            for q in range(k):
                before = jnp.where(keys[q] == keys[k], q, before)
            found.append(before)
        return found

    def table_of(keys):
        out = jnp.full((1, 128), len(keys), jnp.int32)
        for k, key in enumerate(keys):
            out = jnp.where(lanes == key, k, out)
        return out

    row_at = [row_block(k) for k in range(T)]
    for k, before in enumerate(last_of(row_at)):
        prev_s[0, k] = before
    table_v[...] = jnp.zeros_like(table_v)
    table_v[0:1, :] = table_of(row_at)
    pd[T] = jnp.zeros((NV, B), jnp.float32)
    pm[2 * T] = jnp.zeros((NV, B), jnp.float32)

    got("zl")
    send_y(1)

    stages = ((cx_peer, x * 2 + co), (z_peer, zh * 2 + zl), (y_peer, y))

    def share(name, buf, stage, value):
        peer, me = stages[stage]
        buf[stage, me] = value
        for d in (4, 3, 5, 2, 6, 1, 7):
            go((name, stage, d), buf.at[stage, me], buf.at[stage, me], peer(d))

    def shared(name, buf, stage):
        for d in (4, 3, 5, 2, 6, 1, 7):
            got(name, stage, d)
        total = buf[stage, 0]
        for q in range(1, 8):
            total = total + buf[stage, q]
        return total

    arrived_z()
    got("codes")
    local["codes"] = pltpu.make_async_copy(other_v, other_s, local_sem.at[0])
    local["codes"].start()
    arrived_x(0)
    arrived_y2(0)
    for name in ("dirn", "dimg"):
        local.pop(name).wait()
    residual = cat(rbuf.at[c])
    span = jnp.concatenate([own_cd[0:8, :], residual, own_cd[8:16, :]], 0)
    known = jnp.concatenate([cimg[...], jnp.zeros_like(residual), dimg[...], span], 0)
    first = jnp.concatenate([dot(span, known, NT), jnp.zeros((24, 80), jnp.float32)], 1)

    share("early", early, 0, first)
    got("zf", 1)
    send_x(2)
    got("zf", 3)
    send_x(3)
    arrived_y2(1)
    for d in (1, 3):
        go(("spz", d), own_cd, spz.at[d - 1], at(dz=d))
    go(("spl",), own_cd, spl, at(dzl=1))
    arrived_x(1)
    local.pop("codes").wait()
    other_codes = [other_s[0, k] for k in range(T)]
    keys = [jnp.where(code >> 7 == co, code & 127, -1 - k) for k, code in enumerate(codes + other_codes)]
    for k, before in enumerate(last_of(keys)):
        prev_s[1, k] = before
    table_v[1:2, :] = table_of(keys)
    local["table"] = pltpu.make_async_copy(table_v, table_s, local_sem.at[1])
    local["table"].start()
    share("early", early, 2, shared("early", early, 0))
    arrived_x(2)
    arrived_x(3)
    for k in range(T):
        pack[k] = cbuf[other_codes[k] & 127]
    go(("need",), pack, given, at(dco=1))
    go(("spz", 2), own_cd, spz.at[1], at(dz=2))
    local.pop("tiles").wait()
    local.pop("table").wait()
    got("need")

    for k in range(T):
        source = jnp.where(codes[k] >> 7 == co, cbuf[codes[k] & 127], given[k])
        product = split_dot(source, tiles[list_s[2, 0, 0, k]], NT)
        pd[k] = jnp.where(k < live, product, 0.0) + pd[prev_s[0, k]]

    def fill_m(xs):
        def step(q, carry):
            mbuf[xs * 32 + q] = pm[table_s[1, xs * 32 + q]]
            return carry

        lax.fori_loop(0, 32, step, 0, unroll=8)

    def fill_d(q, carry):
        dbuf[q // 8, q % 8] = pd[table_s[0, q]]
        return carry

    def add(ref, *others):
        total = ref[...]
        for other in others:
            total = total + other[...]
        ref[...] = total

    lax.fori_loop(0, 128, fill_d, 0, unroll=8)

    def dpiece(dy, p):
        return dbuf.at[((y + dy) % 8) * 2 + (zl + p) % 2]

    def send_r(step, hops, at_y, way, p, buf):
        go((step, way, p), dpiece(at_y * way, p), buf.at[(1 - way) // 2, p], at(dy=hops * way))

    for way in (1, -1):
        send_r("r3", 1, 3, way, (1 + way) // 2, ry3)
    for way in (1, -1):
        w = (1 - way) // 2
        go(("r4", way), dpiece(4, w), ry4.at[w], at(dy=2 * way))
        send_r("r3", 1, 3, way, w, ry3)

    for way in (1, -1):
        for p in (0, 1):
            got("y1", way, p)
            got("y3", way, p)
        got("y4", way)
    for k in range(T):
        i = row_block(k)
        product = split_dot(rbuf[i >> 3, i & 7], tiles[list_s[2, 0, 0, k]], NN)
        raw[k] = jnp.where(k < live, product, 0.0)
    go(("raw",), raw.at[pl.ds(0, T)], raw.at[pl.ds(T, T)], at(dco=1))
    for way in (1, -1):
        p = (1 + way) // 2
        got("r3", way, p)
        add(dpiece(2 * way, p), ry3.at[(1 - way) // 2, p])
        send_r("r2", 2, 2, way, p, ry2)

    def mpart(dx, first, size):
        return mbuf.at[pl.ds(((x + dx) % 4) * 32 + first, size)]

    got("raw")
    for k in range(2 * T):
        pm[k] = raw[k] + pm[prev_s[1, k]]
    for e in (2, 1, 3, 0):
        fill_m((x + e) % 4)
        if e == 2:
            for d in (1, 3):
                go(("zx", d), mpart(2, 8 * pos[d], 8), zx.at[d // 2], at(dz=-d))
            go(("rx2", 3), mpart(2, 24, 8), rx2.at[1], at(dx=2))
        elif e:
            go(("rx", e), mpart(e, 0, 32), rx.at[e // 2], at(dx=e))
    for way in (1, -1):
        w = (1 - way) // 2
        for p in (0, 1):
            send_r("r1", 1, 1, way, p, ry1)
    got("spl")
    share("early", early, 1, shared("early", early, 2))
    far = mpart(2, 0, 8)
    for d in (1, 3):
        got("zx", d)
    add(far, zx.at[0], zx.at[1])
    go(("rx2", 0), far, rx2.at[0], at(dx=2))

    for way in (1, -1):
        w = (1 - way) // 2
        got("r3", way, w)
        got("r4", way)
        add(dpiece(2 * way, w), ry3.at[w, w], ry4.at[w])
        send_r("r2", 2, 2, way, w, ry2)

    total = shared("early", early, 1)
    at_row = lax.broadcasted_iota(jnp.int32, (24, 24), 0)
    at_col = lax.broadcasted_iota(jnp.int32, (24, 24), 1)
    eye = jnp.where(at_row == at_col, 1.0, 0.0).astype(jnp.float32)
    left, inverse = total[:, 24:48], eye
    for k in range(24):
        root = jnp.sqrt(left[k : k + 1, k : k + 1])
        row = left[k : k + 1, :] / root
        row_inverse = inverse[k : k + 1, :] / root
        factor = left[:, k : k + 1] / root
        left = jnp.where(at_row > k, left - factor * row, jnp.where(at_row == k, row, left))
        inverse = jnp.where(
            at_row > k, inverse - factor * row_inverse, jnp.where(at_row == k, row_inverse, inverse)
        )
    white_known = dot(dot(inverse, total[:, 0:24], NN), inverse, NT)

    for d in (1, 2, 3):
        got("spz", d)
    for e in (1, 3):
        got("rx", e)
    for q in (0, 3):
        got("rx2", q)
    add(mpart(0, 0, 32), rx.at[0], rx.at[1])
    add(mpart(0, 0, 8), rx2.at[0])
    add(mpart(0, 24, 8), rx2.at[1])
    for d in (2, 1, 3):
        go(("rz", d), mpart(0, 8 * pos[d], 8), rz.at[d - 1], at(dz=-d))
    for way in (1, -1):
        for p in (0, 1):
            got("r1", way, p)
            got("r2", way, p)
    for p in (0, 1):
        add(dpiece(0, p), ry1.at[0, p], ry1.at[1, p], ry2.at[0, p], ry2.at[1, p])
    other_c = y * 2 + (1 - zl)
    go(("rzl",), dbuf.at[other_c], rzl, at(dzl=1))

    local.pop("en").wait()
    for s in range(SUB):
        cols = slice(s * B, (s + 1) * B)
        applied[:, cols] = en[:, cols] * rbuf[c, s] + (dbuf[c, s] + mbuf[x * 32 + s])

    def partial_gram(image, own_span, res):
        return dot(image, jnp.concatenate([own_span[0:8, :], res, own_span[8:16, :]], 0), NT)

    gram = partial_gram(applied[...], own_cd, cat(rbuf.at[c]))
    gram = gram + partial_gram(cat(dbuf.at[other_c]), spl, cat(rbuf.at[other_c]))
    for d in (1, 2, 3):
        gram = gram + partial_gram(cat(mpart(0, 8 * pos[d], 8)), spz.at[d - 1], cat(cpart(0, 8 * pos[d], 8)))
    gram = jnp.concatenate([gram, jnp.zeros((NV, 104), jnp.float32)], 1)

    share("late", late, 0, gram)
    share("late", late, 2, shared("late", late, 0))
    gram = shared("late", late, 2)
    share("late", late, 1, gram)

    for d in (1, 3, 2):
        got("rz", d)
    got("rzl")
    for s in range(SUB):
        cols = slice(s * B, (s + 1) * B)
        applied[:, cols] = applied[:, cols] + (rzl[s] + (rz[0, s] + rz[1, s] + rz[2, s]))
    gram = shared("late", late, 1)[:, 0:24]

    white_all = white_known + dot(inverse[:, 8:16], dot(gram, inverse, NT), NN)
    whitened = 0.5 * (white_all + dot(white_all, eye, TN))
    white[...] = 0.5 * (whitened + dot(whitened, eye, TN))

    for copy in copies.values():
        copy.wait_send()


def finish(applied, white, applied_out, white_out, sems):
    first = pltpu.make_async_copy(applied, applied_out, sems.at[0])
    second = pltpu.make_async_copy(white, white_out, sems.at[1])
    first.start()
    second.start()
    first.wait()
    second.wait()


def body(
    tile_data, tile_list, tile_count, current, current_image, direction, direction_image,
    energies, precond, ritz_prev,
):
    vmem = pl.BlockSpec(memory_space=pltpu.VMEM)
    hbm = pl.BlockSpec(memory_space=pltpu.HBM)
    f32 = jnp.float32
    n_ids = len(IDS)
    applied, white = pl.pallas_call(
        kernel,
        out_shape=(pltpu.VMEM(current.shape, f32), pltpu.VMEM((24, 24), f32)),
        in_specs=[hbm] * 10,
        out_specs=(vmem, vmem),
        scratch_shapes=[
            pltpu.SMEM(tile_list.shape, jnp.int32),
            pltpu.SMEM((1, 1), jnp.int32),
            pltpu.VMEM((2 * NV, SUB * B), f32),
            pltpu.VMEM(current.shape, f32),
            pltpu.VMEM(current.shape, f32),
            pltpu.VMEM((1, SUB * B), f32),
            pltpu.VMEM((1, SUB * B), f32),
            pltpu.SMEM((NV,), f32),
            pltpu.VMEM((T, B, B), jnp.bfloat16),
            pltpu.VMEM((16, SUB, NV, B), f32),
            pltpu.VMEM((XN * ZH * SUB, NV, B), f32),
            pltpu.VMEM((16, SUB, NV, B), f32),
            pltpu.VMEM((XN * ZH * SUB, NV, B), f32),
            pltpu.VMEM((2, 2, SUB, NV, B), f32),
            pltpu.VMEM((2, 2, SUB, NV, B), f32),
            pltpu.VMEM((2, 2, SUB, NV, B), f32),
            pltpu.VMEM((2, SUB, NV, B), f32),
            pltpu.VMEM((2, ZH * SUB, NV, B), f32),
            pltpu.VMEM((2, SUB, NV, B), f32),
            pltpu.VMEM((2, SUB, NV, B), f32),
            pltpu.VMEM((3, SUB, NV, B), f32),
            pltpu.VMEM((SUB, NV, B), f32),
            pltpu.VMEM((3, 2 * NV, SUB * B), f32),
            pltpu.VMEM((2 * NV, SUB * B), f32),
            pltpu.VMEM((T + 1, NV, B), f32),
            pltpu.VMEM((2 * T, NV, B), f32),
            pltpu.VMEM((2 * T + 1, NV, B), f32),
            pltpu.VMEM((T, NV, B), f32),
            pltpu.VMEM((T, NV, B), f32),
            pltpu.VMEM((3, 8, 24, 128), f32),
            pltpu.VMEM((3, 8, NV, 128), f32),
            pltpu.VMEM((8, 128), jnp.int32),
            pltpu.SMEM((8, 128), jnp.int32),
            pltpu.SMEM((2, 2 * T), jnp.int32),
            pltpu.VMEM((8, 128), jnp.int32),
            pltpu.VMEM((8, 128), jnp.int32),
            pltpu.SMEM((8, 128), jnp.int32),
            pltpu.SemaphoreType.DMA((n_ids,)),
            pltpu.SemaphoreType.DMA((n_ids,)),
            pltpu.SemaphoreType.DMA((12,)),
        ],
        compiler_params=pltpu.CompilerParams(
            collective_id=0, has_side_effects=True, vmem_limit_bytes=60 * 1024 * 1024
        ),
        name="lobpcg_step",
    )(
        tile_data, tile_list, tile_count, current, current_image, direction, direction_image,
        energies.reshape(1, -1), precond.reshape(1, -1), ritz_prev,
    )
    return (applied, white)


def solution(mesh):
    in_specs = (
        P("row", "col", None, None, None),
        P(None, "row", "col", None),
        P("row", "col"),
        P(None, ("row", "col")),
        P(None, ("row", "col")),
        P(None, ("row", "col")),
        P(None, ("row", "col")),
        P(("row", "col")),
        P(("row", "col")),
        P(),
    )
    out_specs = (P(None, ("row", "col")), P())
    return jax.shard_map(body, mesh=mesh, in_specs=in_specs, out_specs=out_specs, check_vma=False)
```
